32 devices in a mesh: rep: 2 (over x), grp: 4 (over y, core), exp: 4 (over z).
Axes of the slice: x: 2, y: 2, z: 4, core: 2. Of those that a mesh axis runs over, the one named last changes fastest.
Arguments:
- tokens: bfloat16 [512, 7168], P(('rep', 'grp')), parts along dimension 0, may hold values from -6 to 6
- group_ids: int32 [512, 2], P(('rep', 'grp')), parts along dimension 0, may hold values from 0 to 3, all different within a row; in each aligned block of 64 rows (0 to 63, 64 to 127, ...) at most 48 rows name the same one
- gates: bfloat16 [512, 4], P(('rep', 'grp')), parts along dimension 0, may hold values from 0.19921875 to 1
- w_in: bfloat16 [8, 7168, 2, 1024], P('grp', None, None, 'exp'), may hold values from -0.0625 to 0.0625
- w_down: bfloat16 [8, 1024, 7168], P('grp', 'exp'), may hold values from -0.1875 to 0.1875
Outputs:
- mixed: bfloat16 [512, 7168], P(('rep', 'grp', 'exp')), parts along dimension 0
The draws below stay inside these ranges and needn't reach their ends.
There are 2 independent parts, one for each index of `rep`. The reference program is written for one: setup_inputs(seed, part) draws one part's arguments, and reference() takes and returns one part's arrays. A program takes and returns all parts, laid end to end along the dimension named above; an argument that names none is the same for every part. Nothing has to cross between parts.
Inputs may be any that keep to these rules, and one draw needn't show every extreme that they name: `group_ids`: each token names 2 different groups. Among the 64 tokens of one index of grp (aligned blocks of rows) no group is named by more than 48 tokens, a bound that some block reaches.
All inputs are finite; a program needn't handle non-finite values.
Results may differ from the reference program's by a relative error of at most 0.012.
Values may be sent and summed in bfloat16 or wider, within the bound.
No kernel may reach another device: no remote copies, remote signals or barrier semaphores. Data moves between devices by JAX's collectives and lax.ppermute only.
A program may use at most 128 MiB of HBM per device.

```python
import math
import jax
import jax.numpy as jnp
import numpy as np
from jax import lax

D = 7168
HID = 1024
TOK_DEV = 64
TOPG = 2
EXPERTS = 8
CAP = 48
TOKENS = 256
N_GRP = 4
N_EXP = 4


def block_scale(own_key, extent, shards, least, largest):
    factor_of, own = 1.0, jax.random.fold_in(own_key, 6)
    for axis_at, blocks in shards:
        heights = jnp.exp(jax.random.uniform(jax.random.fold_in(own, axis_at), (blocks,), jnp.float32, least / len(shards), largest / len(shards)))
        factor_of = factor_of * jnp.repeat(heights, extent[axis_at] // blocks).reshape([-1 if axis == axis_at else 1 for axis in range(len(extent))])
    return factor_of


def assign_block(own_key, own, number, rows, amount, top, reach, lean):
    sequence = jax.random.permutation(own_key, amount)
    heavy_load, common = load_shares(amount, rows * top, reach, lean, True), load_shares(amount, rows * top, reach, lean, False)
    places = jnp.arange(amount)

    def named(lengths, rotation):
        used = int((lengths > 0).sum())
        fixed = max(1, used // 4)
        shifted = fixed + (places - fixed + rotation * (used - fixed)) % max(1, amount - fixed)
        return jnp.zeros((amount,), jnp.int32).at[sequence[jnp.where(places < fixed, places, shifted)]].set(jnp.asarray(lengths, jnp.int32))

    lengths = jnp.where(number % 4 == 0, named(heavy_load, number // 4), named(common, number - number // 4 - 1))
    mixed = jax.random.permutation(jax.random.fold_in(own, 3), amount)
    donor, receiver = mixed[0:amount // 2 * 2:2], mixed[1:amount // 2 * 2:2]
    slack = jnp.minimum(lengths[donor] - 1, reach - lengths[receiver]) // 2
    slack = jnp.where((donor == sequence[0]) | (receiver == sequence[0]) | (lengths[receiver] == 0), 0, jnp.maximum(slack, 0))
    shifted = jax.random.randint(jax.random.fold_in(own, 4), (amount // 2,), 0, 1 << 20) % (slack + 1)
    lengths = lengths.at[donor].add(-shifted).at[receiver].add(shifted)
    labels = jnp.searchsorted(jnp.cumsum(lengths), jnp.arange(rows * top), side="right").astype(jnp.int32)
    table = labels.reshape(top, rows).T
    table = table[jax.random.permutation(jax.random.fold_in(own, 1), rows)]
    rotation = jax.random.randint(jax.random.fold_in(own, 2), (rows, 1), 0, top)
    return jnp.take_along_axis(table, (jnp.arange(top)[None, :] + rotation) % top, axis=1)


def load_shares(count, total, most, lean, full):
    weights = [(1 << 20) // math.isqrt(standing ** lean) + 1 for standing in range(1, count + 1)]
    largest = most if full else min(most, max(-(-total // count), total * weights[0] // sum(weights)))
    least = 1 if total - largest >= count - 1 else 0
    holding, spare = [largest] + [least] * (count - 1), total - largest - least * (count - 1)
    while spare > 0:
        candidates = [i for i in range(1, count) if holding[i] < largest] or [i for i in range(1, count) if holding[i] < most]
        mass, budget = sum([weights[i] for i in candidates]), spare
        for i in candidates:
            more = min(most - holding[i], max(1, budget * weights[i] // mass), spare)
            holding[i] = holding[i] + more
            spare = spare - more
    return np.array(holding)


def noise(key, extent, spread, reach, cuts=(), kind=jnp.bfloat16):
    drawn = jax.random.normal(key, extent, jnp.float32) * spread
    if len(cuts) > 0:
        drawn = block_scale(key, extent, cuts, -0.22, 0.18) * drawn
    return jnp.clip(drawn, min=-reach, max=reach).astype(kind)


def setup_inputs(seed: int = 0, part: int = 0) -> dict:
    key_of = jax.random.split(jax.random.key(seed), 6)
    own_keys = jax.random.split(jax.random.fold_in(key_of[5], part), 6)
    tokens = noise(own_keys[0], (TOKENS, D), 1.0, 6.0, ((0, 4),))
    group_ids_keys = jax.random.split(jax.random.fold_in(own_keys[1], 1), TOKENS // TOK_DEV)
    group_ids_turns = jax.random.permutation(jax.random.fold_in(own_keys[1], 3), TOKENS // TOK_DEV)
    group_ids = jax.vmap(lambda own, number: assign_block(jax.random.fold_in(own_keys[1], 2), own, number, TOK_DEV, N_GRP, TOPG, CAP, 2))(group_ids_keys, group_ids_turns).reshape((TOKENS, TOPG))
    gates = jnp.clip(0.19921875 + 0.80078125 * jax.random.uniform(own_keys[2], (TOKENS, 2 * TOPG), jnp.float32) ** block_scale(own_keys[2], (TOKENS, 2 * TOPG), ((0, 4),), -0.2, 0.2), 0.19921875, 1.0).astype(jnp.bfloat16)
    w_in = noise(key_of[3], (EXPERTS, D, 2, HID), D ** -0.5, 0.0625, ((0, 4), (3, 4)))
    w_down = noise(key_of[4], (EXPERTS, HID, D), HID ** -0.5, 0.1875, ((0, 4), (1, 4)))
    return {"tokens": tokens, "group_ids": group_ids, "gates": gates, "w_in": w_in, "w_down": w_down}


def reference(tokens, group_ids, gates, w_in, w_down):
    token_count = tokens.shape[0]
    slot_count = N_GRP * CAP
    slice_width = HID // N_EXP
    gate_pairs = gates.astype(jnp.float32).reshape(token_count, TOPG, 2)

    def one_group(total, group):
        matches = group_ids == group
        chosen = jnp.any(matches, axis=1)
        weight = jnp.sum(jnp.where(matches[:, :, None], gate_pairs, 0.0), axis=1)
        picked_rows = jnp.nonzero(chosen, size=slot_count, fill_value=0)[0].astype(jnp.int32)
        valid = (jnp.arange(slot_count, dtype=jnp.int32) < jnp.sum(chosen.astype(jnp.int32))).astype(jnp.float32)
        picked = tokens[picked_rows]
        first = (2 * group).astype(jnp.int32)
        inner = lax.dynamic_slice_in_dim(w_in, first, 2, 0)
        outer = lax.dynamic_slice_in_dim(w_down, first, 2, 0)
        partial_value = jnp.zeros((N_EXP, slot_count, D), jnp.float32)
        for member in range(2):
            gate_up = jnp.dot(picked, inner[member].reshape(D, 2 * HID), preferred_element_type=jnp.float32)
            hidden_act = (jax.nn.silu(gate_up[:, :HID]) * gate_up[:, HID:]).astype(jnp.bfloat16)
            pieces = hidden_act.reshape(slot_count, N_EXP, slice_width).transpose(1, 0, 2).astype(jnp.float32)
            slabs = outer[member].reshape(N_EXP, slice_width, D).astype(jnp.float32)
            output_rows = jnp.einsum('xrh,xhd->xrd', pieces, slabs)
            partial_value = partial_value + weight[picked_rows, member][None, :, None] * output_rows
        rounded = lax.optimization_barrier(partial_value.astype(jnp.bfloat16))
        share = jnp.sum(rounded.astype(jnp.float32), axis=0) * valid[:, None]
        return total.at[picked_rows].add(share), None

    start = jnp.zeros((token_count, D), jnp.float32)
    total, unused = lax.scan(one_group, start, jnp.arange(N_GRP, dtype=jnp.int32))
    return total.astype(jnp.bfloat16)
```

```python
import functools

import jax
import jax.numpy as jnp
from jax import lax
from jax.experimental import pallas as pl
from jax.experimental.pallas import tpu as pltpu
from jax.sharding import PartitionSpec as P

F32 = jnp.float32
BF16 = jnp.bfloat16
LANES = 128
VMEM_LIMIT = 40 << 20


def bits_of(count):
    bits = count.bit_length() - 1
    assert 1 << bits == count
    return bits


def bit_reverse(value, bits):
    return sum(((value >> b) & 1) << (bits - 1 - b) for b in range(bits))


def exchange(x, axis, mask):
    return lax.ppermute(x, axis, [(i, i ^ mask) for i in range(lax.axis_size(axis))])


def add(*terms):
    return sum(t.astype(F32) for t in terms).astype(BF16)


def split(total, unit, shares):
    edges, whole = [0], total // unit
    for i in range(len(shares)):
        edges.append(round(whole * sum(shares[: i + 1]) / sum(shares)) * unit)
    return [(a, b - a) for a, b in zip(edges, edges[1:]) if b > a]


def gate_table(group_ids, gates):
    lane = lax.broadcasted_iota(jnp.int32, (group_ids.shape[0], LANES), 1)
    table = jnp.zeros(lane.shape, BF16)
    for k in range(group_ids.shape[1]):
        pair = jnp.where(lane % 2 == 0, gates[:, 2 * k, None], gates[:, 2 * k + 1, None])
        table = jnp.where(lane // 2 == group_ids[:, k, None], pair, table)
    return table


def up_kernel(first, last, blocks, hidden, parts, *refs):
    refs = list(refs)
    place = refs.pop(0) if last else None
    xs = [refs.pop(0) for _ in range(blocks)]
    w_ref = refs.pop(0)
    before = None if first else refs.pop(0)
    tables = [refs.pop(0) for _ in range(blocks)] if last else []
    out_ref = refs.pop(0)
    wide = refs.pop(0)
    acc = refs.pop(0) if last else out_ref
    step = pl.program_id(0)
    depth = xs[0].shape[1]
    rows = xs[0].shape[0]
    halves = hidden // LANES

    @pl.when(step == 0)
    def _():
        acc[...] = jnp.zeros_like(acc) if first else before[...]

    x = jnp.concatenate([ref[...] for ref in xs], axis=0)
    for member in range(2):
        wide[...] = w_ref[member].astype(F32)
        weights = jnp.concatenate(
            [
                wide[pl.ds(2 * t + s, depth, stride=2 * halves), :].astype(BF16)
                for s in range(2)
                for t in range(halves)
            ],
            axis=1,
        )
        acc[member] += jnp.dot(x, weights, preferred_element_type=F32)

    if last:

        @pl.when(step == pl.num_programs(0) - 1)
        def _():
            group, slot = place[0], place[1]
            bits = bits_of(parts)
            part = rows // parts
            lane = lax.broadcasted_iota(jnp.int32, (rows, LANES), 1)
            for position in range(blocks):
                block = bit_reverse(position, bits_of(blocks))
                table = tables[block][...].astype(F32)
                for member in range(2):
                    gate = jnp.sum(
                        jnp.where(lane == 2 * group + member, table, 0.0), axis=1, keepdims=True
                    )
                    both = acc[member, pl.ds(block * rows, rows), :]
                    a, b = both[:, :hidden], both[:, hidden:]
                    acc[member, pl.ds(block * rows, rows), :hidden] = gate * (jax.nn.silu(a) * b)
                    pieces = []
                    for p in range(parts):
                        source = jnp.bitwise_xor(bit_reverse(p, bits), slot)
                        start = pl.multiple_of(block * rows + source * part, part)
                        pieces.append(acc[member, pl.ds(start, part), :hidden])
                    out_ref[pl.ds(position * rows, rows), pl.ds(member * hidden, hidden)] = (
                        jnp.concatenate(pieces, axis=0).astype(BF16)
                    )


def up_step(xs, w_view, before, tables, place, start, width, hidden, parts):
    first, last = before is None, tables is not None
    blocks, rows = len(xs), xs[0].shape[0]
    depth = width
    ratio = w_view.shape[1] // w_view_depth(w_view, hidden)
    steps = width // depth
    offset = start // depth if start % depth == 0 else None
    if offset is None:
        raise ValueError("uneven chunk")
    operands, specs = [], []
    if last:
        operands.append(place)
        specs.append(pl.BlockSpec(memory_space=pltpu.SMEM))
    for x in xs:
        base = offset if x.shape[1] != width else 0
        operands.append(x)
        specs.append(pl.BlockSpec((rows, depth), lambda j, base=base: (0, base + j)))
    operands.append(w_view)
    specs.append(pl.BlockSpec((2, depth * ratio, LANES), lambda j: (0, offset + j, 0)))
    acc_shape = (2, blocks * rows, 2 * hidden)
    if not first:
        operands.append(before)
        specs.append(pl.BlockSpec(acc_shape, lambda j: (0, 0, 0)))
    if last:
        operands += tables
        specs += [pl.BlockSpec((rows, LANES), lambda j: (0, 0))] * blocks
    scratch = [pltpu.VMEM((depth * ratio, LANES), F32)]
    if last:
        scratch.append(pltpu.VMEM(acc_shape, F32))
        out_shape = jax.ShapeDtypeStruct((blocks * rows, 2 * hidden), BF16)
        out_spec = pl.BlockSpec(out_shape.shape, lambda j: (0, 0))
    else:
        out_shape = jax.ShapeDtypeStruct(acc_shape, F32)
        out_spec = pl.BlockSpec(acc_shape, lambda j: (0, 0, 0))
    return pl.pallas_call(
        functools.partial(up_kernel, first, last, blocks, hidden, parts),
        grid=(steps,),
        in_specs=specs,
        out_specs=out_spec,
        out_shape=out_shape,
        scratch_shapes=scratch,
        compiler_params=pltpu.CompilerParams(vmem_limit_bytes=VMEM_LIMIT),
        cost_estimate=pl.CostEstimate(
            flops=8 * blocks * rows * width * hidden,
            bytes_accessed=8 * width * hidden,
            transcendentals=0,
        ),
        name="up_last" if last else "up",
    )(*operands)


def w_view_depth(w_view, hidden):
    return w_view.shape[1] * LANES // (2 * hidden)


def down_kernel(h_ref, w_ref, keep_ref, send_ref):
    out = jnp.dot(h_ref[...], w_ref[...], preferred_element_type=F32).astype(BF16)
    half = keep_ref.shape[0]
    keep_ref[...] = out[:half]
    send_ref[...] = out[half:]


def down_step(hidden_rows, w_flat, start, width, unit):
    rows, depth = hidden_rows.shape
    offset = start // unit
    half = jax.ShapeDtypeStruct((rows // 2, width), BF16)
    spec = pl.BlockSpec((rows // 2, unit), lambda j: (0, j))
    return pl.pallas_call(
        down_kernel,
        grid=(width // unit,),
        in_specs=[
            pl.BlockSpec((rows, depth), lambda j: (0, 0)),
            pl.BlockSpec((depth, unit), lambda j: (0, offset + j)),
        ],
        out_specs=[spec, spec],
        out_shape=[half, half],
        compiler_params=pltpu.CompilerParams(vmem_limit_bytes=VMEM_LIMIT),
        cost_estimate=pl.CostEstimate(
            flops=2 * rows * width * depth, bytes_accessed=2 * width * depth, transcendentals=0
        ),
        name="down",
    )(hidden_rows, w_flat)


def local(tokens, group_ids, gates, w_in, w_down):
    groups, parts = lax.axis_size("grp"), lax.axis_size("exp")
    rows, features = tokens.shape
    hidden = w_in.shape[3]
    group_bits, part_bits = bits_of(groups), bits_of(parts)
    w_view = (
        w_in.reshape(2, features, 2, hidden // LANES, LANES)
        .transpose(0, 1, 3, 2, 4)
        .reshape(2, -1, LANES)
    )
    w_flat = w_down.reshape(2 * hidden, features)
    place = jnp.stack([lax.axis_index("grp"), lax.axis_index("exp")]).astype(jnp.int32)

    def spread(x):
        held = {0: x}
        for bit in reversed(range(group_bits)):
            for r in list(held):
                held[r | 1 << bit] = exchange(held[r], "grp", 1 << bit)
        return held

    beside = exchange(tokens, "grp", 1)
    chunks = split(features, features // 4, [1, 1, 1, 1])
    tables = spread(gate_table(group_ids, gates))
    value = None
    for at, (start, width) in enumerate(chunks):
        held = {0: lax.slice_in_dim(tokens, start, start + width, axis=1)}
        for bit in reversed(range(group_bits)):
            for r in list(held):
                if r or bit:
                    held[r | 1 << bit] = exchange(held[r], "grp", 1 << bit)
        held[0], held[1] = tokens, beside
        last = at == len(chunks) - 1
        value = up_step(
            [held[r] for r in range(groups)],
            w_view,
            value,
            [tables[r] for r in range(groups)] if last else None,
            place,
            start,
            width,
            hidden,
            parts,
        )

    unit = features // 7
    outs = []
    for start, width in split(features, unit, [1, 2, 2, 1, 1]):
        keep, send = down_step(value, w_flat, start, width, unit)
        terms, height = [keep], keep.shape[0]
        terms.append(exchange(send, "grp", 1))
        for axis, bit in [("grp", b) for b in range(1, group_bits)] + [
            ("exp", b) for b in range(part_bits)
        ]:
            height //= 2
            send = add(*[t[height : 2 * height] for t in terms])
            terms.append(exchange(send, axis, 1 << bit))
        outs.append(add(*[t[:height] for t in terms]))
    return jnp.concatenate(outs, axis=1)


def solution(mesh):
    in_specs = (
        P(("rep", "grp"), None),
        P(("rep", "grp"), None),
        P(("rep", "grp"), None),
        P("grp", None, None, "exp"),
        P("grp", "exp", None),
    )
    out_specs = P(("rep", "grp", "exp"), None)
    return jax.shard_map(local, mesh=mesh, in_specs=in_specs, out_specs=out_specs, check_vma=False)
```

```python
import jax
import jax.numpy as jnp
from jax import lax
from jax.experimental import pallas as pl
from jax.experimental.pallas import tpu as pltpu
from jax.sharding import PartitionSpec as P

F32 = jnp.float32
BF16 = jnp.bfloat16
LANES = 128
VMEM_LIMIT = 16 << 20
RUN = 4
FRONT = 4
CHUNKS = [(1, ("zy", "yz"))]
DOWN_SHARES = [1, 1]


def bits_of(count):
    bits = count.bit_length() - 1
    assert 1 << bits == count
    return bits


def bit_reverse(value, bits):
    return sum(((value >> b) & 1) << (bits - 1 - b) for b in range(bits))


def exchange(x, axis, mask):
    return lax.ppermute(x, axis, [(i, i ^ mask) for i in range(lax.axis_size(axis))])


def add(*terms):
    return sum(t.astype(F32) for t in terms).astype(BF16)


def split(total, unit, shares):
    edges, whole = [0], total // unit
    for i in range(len(shares)):
        edges.append(round(whole * sum(shares[: i + 1]) / sum(shares)) * unit)
    return [(a, b - a) for a, b in zip(edges, edges[1:]) if b > a]


def after(x, *earlier):
    return lax.optimization_barrier((x, earlier))[0]


def prepare(tokens, group_ids, gates, relayed):
    rows, top = group_ids.shape
    direct = tokens.shape[1] - 2 * relayed

    def body(tokens_ref, ids_ref, gates_ref, first, second, table_ref, ids, weights, sems):
        start = pl.multiple_of((lax.axis_index("exp") % 2) * relayed, LANES)
        moves = [
            (ids_ref, ids),
            (gates_ref, weights),
            (tokens_ref.at[:, pl.ds(start, relayed)], first),
            (tokens_ref.at[:, pl.ds(2 * relayed, direct)], second.at[:, pl.ds(0, direct)]),
        ]
        copies = [pltpu.make_async_copy(*move, sems.at[i]) for i, move in enumerate(moves)]
        for copy in copies:
            copy.start()
        for copy in copies[:2]:
            copy.wait()
        expert = lax.broadcasted_iota(jnp.int32, (LANES, rows), 0)
        table = jnp.zeros((LANES, rows), F32)
        for k in range(top):
            even = weights[pl.ds(2 * k, 1), :].astype(F32)
            odd = weights[pl.ds(2 * k + 1, 1), :].astype(F32)
            gate = jnp.where(expert % 2 == 0, even, odd)
            table = jnp.where(expert // 2 == ids[pl.ds(k, 1), :], gate, table)
        table = table.T.astype(BF16)
        table_ref[...] = table
        second[:, pl.ds(direct, LANES)] = table
        for copy in copies[2:]:
            copy.wait()

    widths = [relayed, direct + LANES, LANES]
    return pl.pallas_call(
        body,
        in_specs=[whole(pl.ANY)] * 3,
        out_specs=[whole()] * 3,
        out_shape=[jax.ShapeDtypeStruct((rows, width), BF16) for width in widths],
        scratch_shapes=[
            pltpu.VMEM((top, rows), jnp.int32),
            pltpu.VMEM((2 * top, rows), BF16),
            pltpu.SemaphoreType.DMA((4,)),
        ],
        compiler_params=pltpu.CompilerParams(vmem_limit_bytes=VMEM_LIMIT),
        name="prepare",
    )(in_hbm(tokens), in_hbm(group_ids.T), in_hbm(gates.T))


def in_hbm(x):
    return pltpu.with_memory_space_constraint(x, pltpu.HBM)


def whole(memory_space=pltpu.VMEM):
    return pl.BlockSpec(memory_space=memory_space)


def near_step(xs, w_view, before, hidden, depth, first, last):
    rows, ratio = xs[0].shape[0], 2 * hidden // LANES
    halves, steps = hidden // LANES, last - first

    def body(*refs):
        x_refs, refs = refs[: len(xs)], list(refs[len(xs) :])
        w_ref = refs.pop(0)
        before_ref = None if before is None else refs.pop(0)
        clean_ref, acc_ref, held, blocks, wide, sems = refs
        own = [
            pltpu.make_async_copy(
                ref.at[:, pl.ds(first * depth, steps * depth)],
                held.at[pl.ds(i * rows, rows), :],
                sems.at[2 + i],
            )
            for i, ref in enumerate(x_refs)
        ]

        def fetch(step):
            return pltpu.make_async_copy(
                w_ref.at[:, pl.ds((first + step) * depth * ratio, depth * ratio), :],
                blocks.at[step % 2],
                sems.at[step % 2],
            )

        fetch(0).start()
        for copy in own:
            copy.start()
        for step in range(steps):
            if step + 1 < steps:
                fetch(step + 1).start()
            fetch(step).wait()
            at = step * depth
            for member in range(2):
                wide[...] = blocks[step % 2, member].astype(F32)
                for s in range(2):
                    for t in range(halves):
                        column = (2 * member + s) * hidden + t * LANES
                        clean_ref[pl.ds(at, depth), pl.ds(column, LANES)] = wide[
                            pl.ds(2 * t + s, depth, stride=2 * halves), :
                        ].astype(BF16)
            if step == 0:
                for copy in own:
                    copy.wait()
            value = jnp.dot(
                held[:, pl.ds(at, depth)],
                clean_ref[pl.ds(at, depth), :],
                preferred_element_type=F32,
            )
            if step or before is not None:
                value += (acc_ref if step else before_ref)[...]
            acc_ref[...] = value

    operands = [in_hbm(x) for x in (*xs, w_view)] + ([] if before is None else [before])
    return pl.pallas_call(
        body,
        in_specs=[whole(pl.ANY)] * (len(xs) + 1) + [whole()] * (len(operands) - len(xs) - 1),
        out_specs=[whole(), whole()],
        out_shape=[
            jax.ShapeDtypeStruct((steps * depth, 4 * hidden), BF16),
            jax.ShapeDtypeStruct((len(xs) * rows, 4 * hidden), F32),
        ],
        scratch_shapes=[
            pltpu.VMEM((len(xs) * rows, steps * depth), BF16),
            pltpu.VMEM((2, 2, depth * ratio, LANES), BF16),
            pltpu.VMEM((depth * ratio, LANES), F32),
            pltpu.SemaphoreType.DMA((2 + len(xs),)),
        ],
        compiler_params=pltpu.CompilerParams(vmem_limit_bytes=VMEM_LIMIT),
        name="near",
    )(*operands)


def far_step(before, blocks, parts):
    rows = blocks[0][0].shape[0]
    count = len(blocks[0])
    cleans = []
    for part in parts:
        if not any(part[2] is c for c in cleans):
            cleans.append(part[2])

    def body(*refs):
        refs, out_ref = list(refs[:-1]), refs[-1]
        value = None if before is None else refs.pop(0)[...]
        clean_refs, refs = refs[: len(cleans)], refs[len(cleans) :]
        for which, column, clean, start, depth, shift in parts:
            clean_ref = clean_refs[[c is clean for c in cleans].index(True)]
            x_refs = refs[which * count : (which + 1) * count]
            if shift:
                start = pl.multiple_of(start + (lax.axis_index("exp") % 2) * shift, LANES)
            x = jnp.concatenate([ref[:, pl.ds(column, depth)] for ref in x_refs], axis=0)
            term = jnp.dot(x, clean_ref[pl.ds(start, depth), :], preferred_element_type=F32)
            value = term if value is None else value + term
        out_ref[...] = value

    operands = ([] if before is None else [before]) + cleans + [x for xs in blocks for x in xs]
    return pl.pallas_call(
        body,
        in_specs=[whole()] * len(operands),
        out_specs=whole(),
        out_shape=jax.ShapeDtypeStruct((count * rows, cleans[0].shape[1]), F32),
        compiler_params=pltpu.CompilerParams(vmem_limit_bytes=VMEM_LIMIT),
        name="far",
    )(*operands)


def activate(acc, tables_ref, hidden):
    rows, group = tables_ref[0].shape[0], lax.axis_index("grp")
    lane = lax.broadcasted_iota(jnp.int32, (rows, LANES), 1)
    blocks = []
    for block, table_ref in enumerate(tables_ref):
        table = table_ref[...].astype(F32)
        members = []
        for member in range(2):
            chosen = jnp.where(lane == 2 * group + member, table, 0.0)
            gate = jnp.sum(chosen, axis=1, keepdims=True)
            both = acc[pl.ds(block * rows, rows), pl.ds(2 * member * hidden, 2 * hidden)]
            a, b = both[:, :hidden], both[:, hidden:]
            members.append(gate * (jax.nn.silu(a) * b))
        blocks.append(jnp.concatenate(members, axis=1))
    return jnp.concatenate(blocks, axis=0)


def table_specs(tables):
    return [
        pl.BlockSpec((t.shape[0], LANES), lambda i, c=t.shape[1] // LANES - 1: (0, c))
        for t in tables
    ]


def near_gated(acc, tables, hidden):
    def body(acc_ref, *refs):
        refs[-1][...] = activate(acc_ref, refs[:-1], hidden)

    return pl.pallas_call(
        body,
        grid=(1,),
        in_specs=[whole()] + table_specs(tables),
        out_specs=whole(),
        out_shape=jax.ShapeDtypeStruct((acc.shape[0], 2 * hidden), F32),
        compiler_params=pltpu.CompilerParams(vmem_limit_bytes=VMEM_LIMIT),
        name="near_gated",
    )(acc, *tables)


def far_gated(near_rows, acc, tables, hidden, plans, order):
    rows, count = tables[0].shape[0], near_rows.shape[0]
    total = count + acc.shape[0]
    parts = 1 << sum(axis == "exp" for axis, _ in plans[0][0])
    part, bits = rows // parts, len(plans[0][0])
    at_of = {r: i for i, r in enumerate(order)}

    def body(near_ref, acc_ref, *refs):
        outs, work = refs[len(tables) : -1], refs[-1]
        work[pl.ds(0, count), :] = near_ref[...]
        work[pl.ds(count, total - count), :] = activate(acc_ref, refs[: len(tables)], hidden)
        core, slot = lax.axis_index("grp") % 2, lax.axis_index("exp")
        for routes, out_ref in zip(plans, outs):
            for other in range(2):
                owner = (core + other) % 2
                pieces = []
                for p in range(1 << bits):
                    starts = []
                    for stages in routes:
                        rel = {"grp": other, "exp": 0}
                        for k, (axis, bit) in enumerate(stages):
                            rel[axis] |= ((p >> (bits - 1 - k)) & 1) << bit
                        place = jnp.bitwise_xor(slot, rel["exp"]) * part
                        starts.append(at_of[rel["grp"]] * rows + place)
                    start = jnp.where(owner == 0, *starts)
                    pieces.append(work[pl.ds(pl.multiple_of(start, part), part), :])
                out_ref[pl.ds(other * (total // 2), total // 2), :] = jnp.concatenate(
                    pieces, axis=0
                ).astype(BF16)

    return pl.pallas_call(
        body,
        grid=(1,),
        in_specs=[whole(), whole()] + table_specs(tables),
        out_specs=[whole() for _ in plans],
        out_shape=[jax.ShapeDtypeStruct((total, 2 * hidden), BF16) for _ in plans],
        scratch_shapes=[pltpu.VMEM((total, 2 * hidden), F32)],
        compiler_params=pltpu.CompilerParams(vmem_limit_bytes=VMEM_LIMIT),
        name="far_gated",
    )(near_rows, acc, *tables)


def load(x):
    def body(x_ref, out_ref, sem):
        copy = pltpu.make_async_copy(x_ref, out_ref, sem)
        copy.start()
        copy.wait()

    return pl.pallas_call(
        body,
        in_specs=[whole(pl.ANY)],
        out_specs=whole(),
        out_shape=jax.ShapeDtypeStruct(x.shape, x.dtype),
        scratch_shapes=[pltpu.SemaphoreType.DMA(())],
        compiler_params=pltpu.CompilerParams(vmem_limit_bytes=VMEM_LIMIT),
        name="load",
    )(in_hbm(x))


def down_step(hidden_rows, w_flat, first, count, start, width):
    def body(h_ref, w_ref, out_ref):
        out_ref[...] = jnp.dot(
            h_ref[pl.ds(first, count), :],
            w_ref[:, pl.ds(start, width)],
            preferred_element_type=F32,
        ).astype(BF16)

    return pl.pallas_call(
        body,
        in_specs=[whole(), whole()],
        out_specs=whole(),
        out_shape=jax.ShapeDtypeStruct((count, width), BF16),
        compiler_params=pltpu.CompilerParams(vmem_limit_bytes=VMEM_LIMIT),
        name="down",
    )(hidden_rows, w_flat)


def local(tokens, group_ids, gates, w_in, w_down):
    groups, parts = lax.axis_size("grp"), lax.axis_size("exp")
    rows, features = tokens.shape
    hidden = w_in.shape[3]
    group_bits, part_bits = bits_of(groups), bits_of(parts)
    w_view = (
        w_in.reshape(2, features, 2, hidden // LANES, LANES)
        .transpose(0, 1, 3, 2, 4)
        .reshape(2, -1, LANES)
    )
    w_flat = w_down.reshape(2 * hidden, features)
    unit = features // 7

    def far(x):
        held = {0: x}
        for bit in reversed(range(1, group_bits)):
            for r in list(held):
                held[r | 1 << bit] = exchange(held[r], "grp", 1 << bit)
        return [held[r] for r in range(2, groups, 2)]

    def both(held):
        return held + [exchange(x, "grp", 1) for x in held]

    def both(held):
        return held + [exchange(x, "grp", 1) for x in held]

    run, steps = features // 14 * RUN, features // unit
    beside = exchange(tokens, "grp", 1)
    relayed, direct, table = prepare(tokens, group_ids, gates, run)
    relayed = far(relayed)
    table_beside = exchange(table, "grp", 1)
    clean_front, near_acc = near_step(
        [tokens, beside], w_view, None, hidden, unit, 0, FRONT
    )
    direct = far(after(direct, near_acc))
    relayed, near_acc = lax.optimization_barrier((relayed, near_acc))
    passed = [exchange(x, "exp", 1) for x in relayed]
    clean_back, near_acc = near_step(
        [tokens, beside], w_view, near_acc, hidden, unit, FRONT, steps
    )
    near_rows = near_gated(near_acc, [table, table_beside], hidden)
    far_acc = far_step(None, [both(relayed)], [(0, 0, clean_front, 0, run, run)])
    w_flat = load(after(w_flat, near_rows))
    direct, passed, far_acc, w_flat = lax.optimization_barrier((direct, passed, far_acc, w_flat))
    direct, passed = both(direct), both(passed)
    middle = FRONT * unit - 2 * run
    pieces = [
        (0, 0, clean_front, 2 * run, middle, 0),
        (0, middle, clean_back, 0, features - FRONT * unit, 0),
        (1, 0, clean_front, run, run, -run),
    ]
    pieces = [piece for piece in pieces if piece[4]]
    far_acc = far_step(far_acc, [direct, passed], pieces)

    grp_stages = [("grp", b) for b in range(1, group_bits)]
    exp_stages = [("exp", b) for b in range(part_bits)]
    by_name = {"zy": exp_stages + grp_stages, "yz": grp_stages + exp_stages}
    plans = [[by_name[name] for name in names] for _, names in CHUNKS]
    order = [0, 1] + list(range(2, groups, 2)) + list(range(3, groups, 2))
    all_rows = far_gated(near_rows, far_acc, direct, hidden, plans, order)

    def turn(x, routes, stage):
        pairs = []
        for g in range(groups):
            for e in range(parts):
                axis, bit = routes[g % 2][stage]
                to_g, to_e = (g ^ 1 << bit, e) if axis == "grp" else (g, e ^ 1 << bit)
                pairs.append((g * parts + e, to_g * parts + to_e))
        return lax.ppermute(x, ("grp", "exp"), pairs)

    state = []
    half = rows * groups // 2
    spans = split(features, features // 28, [share for share, _ in CHUNKS])
    for (start, width), plan_rows in zip(spans, all_rows):
        comes = []
        for offset, piece in split(width, features // 56, DOWN_SHARES):
            send = down_step(plan_rows, w_flat, half, half, start + offset, piece)
            plan_rows = after(plan_rows, send)
            comes.append(exchange(send, "grp", 1))
        keep = down_step(plan_rows, w_flat, 0, half, start, width)
        state.append([keep, jnp.concatenate(comes, axis=1)])
    token = None
    height = rows * groups // 2
    for stage in range(len(grp_stages + exp_stages)):
        height //= 2
        for terms, routes in zip(state, plans):
            back = turn(add(*[t[height : 2 * height] for t in terms]), routes, stage)
            if token is not None:
                back = after(back, token)
            terms.append(back)
            token = back
    return jnp.concatenate([add(*[t[:height] for t in terms]) for terms in state], axis=1)


def solution(mesh):
    in_specs = (
        P(("rep", "grp"), None),
        P(("rep", "grp"), None),
        P(("rep", "grp"), None),
        P("grp", None, None, "exp"),
        P("grp", "exp", None),
    )
    out_specs = P(("rep", "grp", "exp"), None)
    return jax.shard_map(local, mesh=mesh, in_specs=in_specs, out_specs=out_specs, check_vma=False)
```

```python
import jax
import jax.numpy as jnp
from jax import lax
from jax.experimental import pallas as pl
from jax.experimental.pallas import tpu as pltpu
from jax.sharding import PartitionSpec as P

F32 = jnp.float32
BF16 = jnp.bfloat16
LANES = 128
VMEM_LIMIT = 16 << 20
RUN = 4
FRONT = 3
CHUNKS = [(6, ("zyz", "yz")), (5, ("Zyz", "yZ"))]


def bits_of(count):
    bits = count.bit_length() - 1
    assert 1 << bits == count
    return bits


def bit_reverse(value, bits):
    return sum(((value >> b) & 1) << (bits - 1 - b) for b in range(bits))


def exchange(x, axis, mask):
    return lax.ppermute(x, axis, [(i, i ^ mask) for i in range(lax.axis_size(axis))])


def add(*terms):
    return sum(t.astype(F32) for t in terms).astype(BF16)


def split(total, unit, shares):
    edges, whole = [0], total // unit
    for i in range(len(shares)):
        edges.append(round(whole * sum(shares[: i + 1]) / sum(shares)) * unit)
    return [(a, b - a) for a, b in zip(edges, edges[1:]) if b > a]


def after(x, *earlier):
    return lax.optimization_barrier((x, earlier))[0]


def prepare(tokens, group_ids, gates, relayed):
    rows, top = group_ids.shape
    direct = tokens.shape[1] - 2 * relayed

    def body(tokens_ref, ids_ref, gates_ref, first, second, table_ref, ids, weights, sems):
        start = pl.multiple_of((lax.axis_index("exp") % 2) * relayed, LANES)
        moves = [
            (ids_ref, ids),
            (gates_ref, weights),
            (tokens_ref.at[:, pl.ds(start, relayed)], first),
            (tokens_ref.at[:, pl.ds(2 * relayed, direct)], second.at[:, pl.ds(0, direct)]),
        ]
        copies = [pltpu.make_async_copy(*move, sems.at[i]) for i, move in enumerate(moves)]
        for copy in copies:
            copy.start()
        for copy in copies[:2]:
            copy.wait()
        expert = lax.broadcasted_iota(jnp.int32, (LANES, rows), 0)
        table = jnp.zeros((LANES, rows), F32)
        for k in range(top):
            even = weights[pl.ds(2 * k, 1), :].astype(F32)
            odd = weights[pl.ds(2 * k + 1, 1), :].astype(F32)
            gate = jnp.where(expert % 2 == 0, even, odd)
            table = jnp.where(expert // 2 == ids[pl.ds(k, 1), :], gate, table)
        table = table.T.astype(BF16)
        table_ref[...] = table
        second[:, pl.ds(direct, LANES)] = table
        for copy in copies[2:]:
            copy.wait()

    widths = [relayed, direct + LANES, LANES]
    return pl.pallas_call(
        body,
        in_specs=[whole(pl.ANY)] * 3,
        out_specs=[whole()] * 3,
        out_shape=[jax.ShapeDtypeStruct((rows, width), BF16) for width in widths],
        scratch_shapes=[
            pltpu.VMEM((top, rows), jnp.int32),
            pltpu.VMEM((2 * top, rows), BF16),
            pltpu.SemaphoreType.DMA((4,)),
        ],
        compiler_params=pltpu.CompilerParams(vmem_limit_bytes=VMEM_LIMIT),
        name="prepare",
    )(in_hbm(tokens), in_hbm(group_ids.T), in_hbm(gates.T))


def in_hbm(x):
    return pltpu.with_memory_space_constraint(x, pltpu.HBM)


def whole(memory_space=pltpu.VMEM):
    return pl.BlockSpec(memory_space=memory_space)


def near_step(xs, w_view, before, hidden, depth, first, last, extra=None, spans=()):
    rows, ratio = xs[0].shape[0], 2 * hidden // LANES
    features = w_view.shape[1] // ratio
    halves, steps = hidden // LANES, last - first

    def body(*refs):
        x_refs, refs = refs[: len(xs)], list(refs[len(xs) :])
        w_ref = refs.pop(0)
        if extra is not None:
            extra_ref = refs.pop(0)
        if before is not None:
            before_ref, _ = refs.pop(0), refs.pop(0)
        acc_ref, clean_ref = refs.pop(0), refs.pop(0)
        extra_outs = [refs.pop(0) for _ in spans]
        held, blocks, sems = refs
        own = [
            pltpu.make_async_copy(
                ref.at[:, pl.ds(first * depth, steps * depth)],
                held.at[pl.ds(i * rows, rows), :],
                sems.at[i],
            )
            for i, ref in enumerate(x_refs)
        ]

        def fetch(step):
            return pltpu.make_async_copy(
                w_ref.at[:, pl.ds((first + step) * depth * ratio, depth * ratio), :],
                blocks.at[step],
                sems.at[len(xs) + step],
            )

        pieces = [
            pltpu.make_async_copy(
                extra_ref.at[:, pl.ds(*span)], out, sems.at[len(xs) + steps + i]
            )
            for i, (span, out) in enumerate(zip(spans, extra_outs))
        ]
        fetch(0).start()
        for copy in own:
            copy.start()
        for step in range(1, steps):
            fetch(step).start()
        for copy in pieces:
            copy.start()
        for step in range(steps):
            fetch(step).wait()
            here = pl.ds((first + step) * depth, depth)
            for member in range(2):
                for s in range(2):
                    for t in range(halves):
                        column = (2 * member + s) * hidden + t * LANES
                        clean_ref[here, pl.ds(column, LANES)] = blocks[
                            step, member, pl.ds(2 * t + s, depth, stride=2 * halves), :
                        ]
            if step == 0:
                for copy in own:
                    copy.wait()
            value = jnp.dot(
                held[:, pl.ds(step * depth, depth)],
                clean_ref[here, :],
                preferred_element_type=F32,
            )
            if step or before is not None:
                value += (acc_ref if step else before_ref)[...]
            acc_ref[...] = value
        for copy in pieces:
            copy.wait()

    operands = [in_hbm(xs[0]), *xs[1:], in_hbm(w_view)]
    specs = [whole(pl.ANY)] * len(operands)
    if extra is not None:
        operands.append(in_hbm(extra))
        specs.append(whole(pl.ANY))
    aliases = {}
    if before is not None:
        aliases = {len(operands): 0, len(operands) + 1: 1}
        operands += before
        specs += [whole()] * 2
    shapes = [
        jax.ShapeDtypeStruct((len(xs) * rows, 4 * hidden), F32),
        jax.ShapeDtypeStruct((features, 4 * hidden), BF16),
    ]
    for _, width in spans:
        shapes.append(jax.ShapeDtypeStruct((extra.shape[0], width), extra.dtype))
    return pl.pallas_call(
        body,
        in_specs=specs,
        out_specs=[whole()] * len(shapes),
        out_shape=shapes,
        input_output_aliases=aliases,
        scratch_shapes=[
            pltpu.VMEM((len(xs) * rows, steps * depth), BF16),
            pltpu.VMEM((steps, 2, depth * ratio, LANES), BF16),
            pltpu.SemaphoreType.DMA((len(xs) + steps + len(spans),)),
        ],
        compiler_params=pltpu.CompilerParams(vmem_limit_bytes=VMEM_LIMIT),
        name="near",
    )(*operands)


def far_step(before, blocks, parts):
    rows = blocks[0][0].shape[0]
    count = len(blocks[0])
    cleans = []
    for part in parts:
        if not any(part[2] is c for c in cleans):
            cleans.append(part[2])

    def body(*refs):
        refs, out_ref = list(refs[:-1]), refs[-1]
        value = None if before is None else refs.pop(0)[...]
        clean_refs, refs = refs[: len(cleans)], refs[len(cleans) :]
        for which, column, clean, start, depth, shift in parts:
            clean_ref = clean_refs[[c is clean for c in cleans].index(True)]
            x_refs = refs[which * count : (which + 1) * count]
            if shift:
                start = pl.multiple_of(start + (lax.axis_index("exp") % 2) * shift, LANES)
            x = jnp.concatenate([ref[:, pl.ds(column, depth)] for ref in x_refs], axis=0)
            term = jnp.dot(x, clean_ref[pl.ds(start, depth), :], preferred_element_type=F32)
            value = term if value is None else value + term
        out_ref[...] = value

    operands = ([] if before is None else [before]) + cleans + [x for xs in blocks for x in xs]
    return pl.pallas_call(
        body,
        in_specs=[whole()] * len(operands),
        out_specs=whole(),
        out_shape=jax.ShapeDtypeStruct((count * rows, cleans[0].shape[1]), F32),
        compiler_params=pltpu.CompilerParams(vmem_limit_bytes=VMEM_LIMIT),
        name="far",
    )(*operands)


def activate(acc, tables_ref, hidden):
    rows, group = tables_ref[0].shape[0], lax.axis_index("grp")
    lane = lax.broadcasted_iota(jnp.int32, (rows, LANES), 1)
    blocks = []
    for block, table_ref in enumerate(tables_ref):
        table = table_ref[...].astype(F32)
        members = []
        for member in range(2):
            chosen = jnp.where(lane == 2 * group + member, table, 0.0)
            gate = jnp.sum(chosen, axis=1, keepdims=True)
            both = acc[pl.ds(block * rows, rows), pl.ds(2 * member * hidden, 2 * hidden)]
            a, b = both[:, :hidden], both[:, hidden:]
            members.append(gate * (jax.nn.silu(a) * b))
        blocks.append(jnp.concatenate(members, axis=1))
    return jnp.concatenate(blocks, axis=0)


def table_specs(tables):
    return [
        pl.BlockSpec((t.shape[0], LANES), lambda i, c=t.shape[1] // LANES - 1: (0, c))
        for t in tables
    ]


def near_gated(acc, tables, hidden):
    def body(acc_ref, *refs):
        refs[-1][...] = activate(acc_ref, refs[:-1], hidden)

    return pl.pallas_call(
        body,
        grid=(1,),
        in_specs=[whole()] + table_specs(tables),
        out_specs=whole(),
        out_shape=jax.ShapeDtypeStruct((acc.shape[0], 2 * hidden), F32),
        compiler_params=pltpu.CompilerParams(vmem_limit_bytes=VMEM_LIMIT),
        name="near_gated",
    )(acc, *tables)


def far_gated(near_rows, acc, tables, hidden, plans, order):
    rows, count = tables[0].shape[0], near_rows.shape[0]
    total = count + acc.shape[0]
    parts = 1 << sum(axis == "exp" for axis, _ in plans[0][0])
    part, bits = rows // parts, len(plans[0][0])
    at_of = {r: i for i, r in enumerate(order)}

    def body(near_ref, acc_ref, *refs):
        outs, work = refs[len(tables) : -1], refs[-1]
        work[pl.ds(0, count), :] = near_ref[...]
        work[pl.ds(count, total - count), :] = activate(acc_ref, refs[: len(tables)], hidden)
        core, slot = lax.axis_index("grp") % 2, lax.axis_index("exp")
        for routes, out_ref in zip(plans, outs):
            for other in range(2):
                owner = (core + other) % 2
                pieces = []
                for p in range(1 << bits):
                    starts = []
                    for stages in routes:
                        rel = {"grp": other, "exp": 0}
                        for k, (axis, bit) in enumerate(stages):
                            rel[axis] |= ((p >> (bits - 1 - k)) & 1) << bit
                        place = jnp.bitwise_xor(slot, rel["exp"]) * part
                        starts.append(at_of[rel["grp"]] * rows + place)
                    start = jnp.where(owner == 0, *starts)
                    pieces.append(work[pl.ds(pl.multiple_of(start, part), part), :])
                out_ref[pl.ds(other * (total // 2), total // 2), :] = jnp.concatenate(
                    pieces, axis=0
                ).astype(BF16)

    return pl.pallas_call(
        body,
        grid=(1,),
        in_specs=[whole(), whole()] + table_specs(tables),
        out_specs=[whole() for _ in plans],
        out_shape=[jax.ShapeDtypeStruct((total, 2 * hidden), BF16) for _ in plans],
        scratch_shapes=[pltpu.VMEM((total, 2 * hidden), F32)],
        compiler_params=pltpu.CompilerParams(vmem_limit_bytes=VMEM_LIMIT),
        name="far_gated",
    )(near_rows, acc, *tables)


def down_step(hidden_rows, weights, first, count):
    def body(h_ref, w_ref, out_ref):
        out_ref[...] = jnp.dot(
            h_ref[pl.ds(first, count), :], w_ref[...], preferred_element_type=F32
        ).astype(BF16)

    return pl.pallas_call(
        body,
        in_specs=[whole(), whole()],
        out_specs=whole(),
        out_shape=jax.ShapeDtypeStruct((count, weights.shape[1]), BF16),
        compiler_params=pltpu.CompilerParams(vmem_limit_bytes=VMEM_LIMIT),
        name="down",
    )(hidden_rows, weights)


def local(tokens, group_ids, gates, w_in, w_down):
    groups, parts = lax.axis_size("grp"), lax.axis_size("exp")
    rows, features = tokens.shape
    hidden = w_in.shape[3]
    group_bits, part_bits = bits_of(groups), bits_of(parts)
    w_view = (
        w_in.reshape(2, features, 2, hidden // LANES, LANES)
        .transpose(0, 1, 3, 2, 4)
        .reshape(2, -1, LANES)
    )
    w_flat = w_down.reshape(2 * hidden, features)
    unit = features // 7

    def far(x):
        held = {0: x}
        for bit in reversed(range(1, group_bits)):
            for r in list(held):
                held[r | 1 << bit] = exchange(held[r], "grp", 1 << bit)
        return [held[r] for r in range(2, groups, 2)]

    def both(held):
        return held + [exchange(x, "grp", 1) for x in held]

    def both(held):
        return held + [exchange(x, "grp", 1) for x in held]

    run, steps = features // 14 * RUN, features // unit
    beside = exchange(tokens, "grp", 1)
    relayed, direct, table = prepare(tokens, group_ids, gates, run)
    relayed = far(relayed)
    table_beside = exchange(table, "grp", 1)
    held = [tokens, beside]
    spans = split(features, features // 28, [share for share, _ in CHUNKS])
    near = near_step(held, w_view, None, hidden, unit, 0, FRONT)
    direct = far(after(direct, near[0]))
    relayed, near = lax.optimization_barrier((relayed, near))
    passed = [exchange(x, "exp", 1) for x in relayed]
    near_acc, clean, *w_flats = near_step(
        held, w_view, near, hidden, unit, FRONT, steps, w_flat, spans
    )
    near_rows = near_gated(near_acc, [table, table_beside], hidden)
    far_acc = far_step(None, [both(relayed)], [(0, 0, clean, 0, run, run)])
    direct, passed, far_acc, near_rows = lax.optimization_barrier(
        (direct, passed, far_acc, near_rows)
    )
    passed, direct = both(passed), both(direct)
    far_acc = far_step(far_acc, [passed], [(0, 0, clean, run, run, -run)])
    direct[-1] = after(direct[-1], far_acc)
    far_acc = far_step(far_acc, [direct], [(0, 0, clean, 2 * run, features - 2 * run, 0)])

    grp_stages = [("grp", b) for b in range(1, group_bits)]
    exp_stages = [("exp", b) for b in range(part_bits)]
    turned = exp_stages[::-1]
    by_name = {
        "yz": grp_stages + exp_stages,
        "yZ": grp_stages + turned,
        "zyz": exp_stages[:1] + grp_stages + exp_stages[1:],
        "Zyz": turned[:1] + grp_stages + turned[1:],
    }
    plans = [[by_name[name] for name in names] for _, names in CHUNKS]
    order = [0, 1] + list(range(2, groups, 2)) + list(range(3, groups, 2))
    all_rows = far_gated(near_rows, far_acc, direct, hidden, plans, order)

    def turn(x, routes, stage):
        pairs = []
        for g in range(groups):
            for e in range(parts):
                axis, bit = routes[g % 2][stage]
                to_g, to_e = (g ^ 1 << bit, e) if axis == "grp" else (g, e ^ 1 << bit)
                pairs.append((g * parts + e, to_g * parts + to_e))
        return lax.ppermute(x, ("grp", "exp"), pairs)

    state = []
    half = rows * groups // 2
    done = None
    for weights, plan_rows in zip(w_flats, all_rows):
        plan_rows = plan_rows if done is None else after(plan_rows, done)
        done = down_step(plan_rows, weights, half, half)
        state.append([exchange(done, "grp", 1)])
    for weights, plan_rows, terms in zip(w_flats, all_rows, state):
        done = down_step(after(plan_rows, done), weights, 0, half)
        terms.append(done)
    send = None
    height = half
    for stage in range(len(grp_stages + exp_stages)):
        height //= 2
        for terms, routes in zip(state, plans):
            if send is not None:
                terms[-1] = after(terms[-1], send)
            send = add(*[t[height : 2 * height] for t in terms])
            terms.append(turn(send, routes, stage))
    outs = []
    for terms in state:
        if outs:
            terms[-1] = after(terms[-1], outs[-1])
        outs.append(add(*[t[:height] for t in terms]))
    return jnp.concatenate(outs, axis=1)


def solution(mesh):
    in_specs = (
        P(("rep", "grp"), None),
        P(("rep", "grp"), None),
        P(("rep", "grp"), None),
        P("grp", None, None, "exp"),
        P("grp", "exp", None),
    )
    out_specs = P(("rep", "grp", "exp"), None)
    return jax.shard_map(local, mesh=mesh, in_specs=in_specs, out_specs=out_specs, check_vma=False)
```

```python
import jax
import jax.numpy as jnp
from jax import lax
from jax.experimental import pallas as pl
from jax.experimental.pallas import tpu as pltpu
from jax.sharding import PartitionSpec as P

F32 = jnp.float32
BF16 = jnp.bfloat16
LANES = 128
VMEM_LIMIT = 16 << 20
NEAR_COST = 3_000_000_000
RUN = 4
FRONT = 3
CHUNKS = [(17, ('yZ', 'zyz')), (11, ('yz', 'Zyz'))]


def bits_of(count):
    bits = count.bit_length() - 1
    assert 1 << bits == count
    return bits


def bit_reverse(value, bits):
    return sum(((value >> b) & 1) << (bits - 1 - b) for b in range(bits))


def exchange(x, axis, mask):
    return lax.ppermute(x, axis, [(i, i ^ mask) for i in range(lax.axis_size(axis))])


def add(*terms):
    return sum(t.astype(F32) for t in terms).astype(BF16)


def split(total, unit, shares):
    edges, whole = [0], total // unit
    for i in range(len(shares)):
        edges.append(round(whole * sum(shares[: i + 1]) / sum(shares)) * unit)
    return [(a, b - a) for a, b in zip(edges, edges[1:]) if b > a]


def after(x, *earlier):
    return lax.optimization_barrier((x, earlier))[0]


def prepare(tokens, group_ids, gates, relayed):
    rows, top = group_ids.shape
    direct = tokens.shape[1] - 2 * relayed

    def body(tokens_ref, ids_ref, gates_ref, first, second, table_ref, ids, weights, sems):
        start = pl.multiple_of((lax.axis_index("exp") % 2) * relayed, LANES)
        moves = [
            (ids_ref, ids),
            (gates_ref, weights),
            (tokens_ref.at[:, pl.ds(start, relayed)], first),
            (tokens_ref.at[:, pl.ds(2 * relayed, direct)], second.at[:, pl.ds(0, direct)]),
        ]
        copies = [pltpu.make_async_copy(*move, sems.at[i]) for i, move in enumerate(moves)]
        for copy in copies:
            copy.start()
        for copy in copies[:2]:
            copy.wait()
        expert = lax.broadcasted_iota(jnp.int32, (LANES, rows), 0)
        table = jnp.zeros((LANES, rows), F32)
        for k in range(top):
            even = weights[pl.ds(2 * k, 1), :].astype(F32)
            odd = weights[pl.ds(2 * k + 1, 1), :].astype(F32)
            gate = jnp.where(expert % 2 == 0, even, odd)
            table = jnp.where(expert // 2 == ids[pl.ds(k, 1), :], gate, table)
        table = table.T.astype(BF16)
        table_ref[...] = table
        second[:, pl.ds(direct, LANES)] = table
        for copy in copies[2:]:
            copy.wait()

    widths = [relayed, direct + LANES, LANES]
    return pl.pallas_call(
        body,
        in_specs=[whole(pl.ANY)] * 3,
        out_specs=[whole()] * 3,
        out_shape=[jax.ShapeDtypeStruct((rows, width), BF16) for width in widths],
        scratch_shapes=[
            pltpu.VMEM((top, rows), jnp.int32),
            pltpu.VMEM((2 * top, rows), BF16),
            pltpu.SemaphoreType.DMA((4,)),
        ],
        compiler_params=pltpu.CompilerParams(vmem_limit_bytes=VMEM_LIMIT),
        name="prepare",
    )(in_hbm(tokens), in_hbm(group_ids.T), in_hbm(gates.T))


def in_hbm(x):
    return pltpu.with_memory_space_constraint(x, pltpu.HBM)


def whole(memory_space=pltpu.VMEM):
    return pl.BlockSpec(memory_space=memory_space)


def near_step(xs, w_view, before, hidden, depth, first, last, extra=None, spans=()):
    rows, ratio = xs[0].shape[0], 2 * hidden // LANES
    features = w_view.shape[1] // ratio
    halves, steps = hidden // LANES, last - first

    def body(*refs):
        x_refs, refs = refs[: len(xs)], list(refs[len(xs) :])
        w_ref = refs.pop(0)
        if extra is not None:
            extra_ref = refs.pop(0)
        if before is not None:
            before_ref, _ = refs.pop(0), refs.pop(0)
        acc_ref, clean_ref = refs.pop(0), refs.pop(0)
        extra_outs = [refs.pop(0) for _ in spans]
        held, blocks, sems = refs
        own = [
            pltpu.make_async_copy(
                ref.at[:, pl.ds(first * depth, steps * depth)],
                held.at[pl.ds(i * rows, rows), :],
                sems.at[i],
            )
            for i, ref in enumerate(x_refs)
        ]

        def fetch(step):
            return pltpu.make_async_copy(
                w_ref.at[:, pl.ds((first + step) * depth * ratio, depth * ratio), :],
                blocks.at[step],
                sems.at[len(xs) + step],
            )

        pieces = [
            pltpu.make_async_copy(
                extra_ref.at[:, pl.ds(*span)], out, sems.at[len(xs) + steps + i]
            )
            for i, (span, out) in enumerate(zip(spans, extra_outs))
        ]
        fetch(0).start()
        for copy in own:
            copy.start()
        for step in range(1, steps):
            fetch(step).start()
        for copy in pieces:
            copy.start()
        for step in range(steps):
            fetch(step).wait()
            here = pl.ds((first + step) * depth, depth)
            for member in range(2):
                for s in range(2):
                    for t in range(halves):
                        column = (2 * member + s) * hidden + t * LANES
                        clean_ref[here, pl.ds(column, LANES)] = blocks[
                            step, member, pl.ds(2 * t + s, depth, stride=2 * halves), :
                        ]
            if step == 0:
                for copy in own:
                    copy.wait()
            value = jnp.dot(
                held[:, pl.ds(step * depth, depth)],
                clean_ref[here, :],
                preferred_element_type=F32,
            )
            if step or before is not None:
                value += (acc_ref if step else before_ref)[...]
            acc_ref[...] = value
        for copy in pieces:
            copy.wait()

    operands = [in_hbm(xs[0]), *xs[1:], in_hbm(w_view)]
    specs = [whole(pl.ANY)] * len(operands)
    if extra is not None:
        operands.append(in_hbm(extra))
        specs.append(whole(pl.ANY))
    aliases = {}
    if before is not None:
        aliases = {len(operands): 0, len(operands) + 1: 1}
        operands += before
        specs += [whole()] * 2
    shapes = [
        jax.ShapeDtypeStruct((len(xs) * rows, 4 * hidden), F32),
        jax.ShapeDtypeStruct((features, 4 * hidden), BF16),
    ]
    for _, width in spans:
        shapes.append(jax.ShapeDtypeStruct((extra.shape[0], width), extra.dtype))
    return pl.pallas_call(
        body,
        in_specs=specs,
        out_specs=[whole()] * len(shapes),
        out_shape=shapes,
        input_output_aliases=aliases,
        scratch_shapes=[
            pltpu.VMEM((len(xs) * rows, steps * depth), BF16),
            pltpu.VMEM((steps, 2, depth * ratio, LANES), BF16),
            pltpu.SemaphoreType.DMA((len(xs) + steps + len(spans),)),
        ],
        compiler_params=pltpu.CompilerParams(vmem_limit_bytes=VMEM_LIMIT),
        cost_estimate=pl.CostEstimate(
            flops=NEAR_COST, bytes_accessed=NEAR_COST // 300, transcendentals=0
        ),
        name="near",
    )(*operands)


def add_far(value, clean_ref, x_refs, parts, count):
    for which, column, start, depth, shift in parts:
        refs = x_refs[which * count : (which + 1) * count]
        if shift:
            start = pl.multiple_of(start + (lax.axis_index("exp") % 2) * shift, LANES)
        x = jnp.concatenate([ref[:, pl.ds(column, depth)] for ref in refs], axis=0)
        term = jnp.dot(x, clean_ref[pl.ds(start, depth), :], preferred_element_type=F32)
        value = term if value is None else value + term
    return value


def far_step(before, clean, blocks, parts):
    rows, count = blocks[0][0].shape[0], len(blocks[0])
    first = [] if before is None else [before]

    def body(*refs):
        value = None if before is None else refs[0][...]
        clean_ref, x_refs = refs[len(first)], refs[len(first) + 1 : -1]
        refs[-1][...] = add_far(value, clean_ref, x_refs, parts, count)

    operands = first + [clean] + [x for xs in blocks for x in xs]
    return pl.pallas_call(
        body,
        in_specs=[whole()] * len(operands),
        out_specs=whole(),
        out_shape=jax.ShapeDtypeStruct((count * rows, clean.shape[1]), F32),
        compiler_params=pltpu.CompilerParams(vmem_limit_bytes=VMEM_LIMIT),
        name="far",
    )(*operands)


def activate(acc, tables_ref, hidden):
    rows, group = tables_ref[0].shape[0], lax.axis_index("grp")
    lane = lax.broadcasted_iota(jnp.int32, (rows, LANES), 1)
    blocks = []
    for block, table_ref in enumerate(tables_ref):
        table = table_ref[...].astype(F32)
        members = []
        for member in range(2):
            chosen = jnp.where(lane == 2 * group + member, table, 0.0)
            gate = jnp.sum(chosen, axis=1, keepdims=True)
            both = acc[pl.ds(block * rows, rows), pl.ds(2 * member * hidden, 2 * hidden)]
            a, b = both[:, :hidden], both[:, hidden:]
            members.append(gate * (jax.nn.silu(a) * b))
        blocks.append(jnp.concatenate(members, axis=1))
    return jnp.concatenate(blocks, axis=0)


def table_specs(tables):
    return [
        pl.BlockSpec((t.shape[0], LANES), lambda i, c=t.shape[1] // LANES - 1: (0, c))
        for t in tables
    ]


def near_gated(acc, tables, hidden):
    def body(acc_ref, *refs):
        refs[-1][...] = activate(acc_ref, refs[:-1], hidden)

    return pl.pallas_call(
        body,
        grid=(1,),
        in_specs=[whole()] + table_specs(tables),
        out_specs=whole(),
        out_shape=jax.ShapeDtypeStruct((acc.shape[0], 2 * hidden), F32),
        compiler_params=pltpu.CompilerParams(vmem_limit_bytes=VMEM_LIMIT),
        name="near_gated",
    )(acc, *tables)


def far_gated(near_rows, acc, clean, blocks, far_parts, tables, hidden, plans, order):
    rows, count = tables[0].shape[0], near_rows.shape[0]
    total = count + acc.shape[0]
    parts = 1 << sum(axis == "exp" for axis, _ in plans[0][0])
    part, bits = rows // parts, len(plans[0][0])
    at_of = {r: i for i, r in enumerate(order)}
    xs = [x for block in blocks for x in block]

    def body(near_ref, acc_ref, clean_ref, *refs):
        x_refs, refs = refs[: len(xs)], refs[len(xs) :]
        table_refs, outs, (work, sums) = refs[: len(tables)], refs[len(tables) : -2], refs[-2:]
        sums[...] = add_far(acc_ref[...], clean_ref, x_refs, far_parts, len(blocks[0]))
        work[pl.ds(0, count), :] = near_ref[...]
        work[pl.ds(count, total - count), :] = activate(sums, table_refs, hidden)
        core, slot = lax.axis_index("grp") % 2, lax.axis_index("exp")
        for routes, out_ref in zip(plans, outs):
            for other in range(2):
                owner = (core + other) % 2
                pieces = []
                for p in range(1 << bits):
                    starts = []
                    for stages in routes:
                        rel = {"grp": other, "exp": 0}
                        for k, (axis, bit) in enumerate(stages):
                            rel[axis] |= ((p >> (bits - 1 - k)) & 1) << bit
                        place = jnp.bitwise_xor(slot, rel["exp"]) * part
                        starts.append(at_of[rel["grp"]] * rows + place)
                    start = jnp.where(owner == 0, *starts)
                    pieces.append(work[pl.ds(pl.multiple_of(start, part), part), :])
                out_ref[pl.ds(other * (total // 2), total // 2), :] = jnp.concatenate(
                    pieces, axis=0
                ).astype(BF16)

    return pl.pallas_call(
        body,
        grid=(1,),
        in_specs=[whole()] * (3 + len(xs)) + table_specs(tables),
        out_specs=[whole() for _ in plans],
        out_shape=[jax.ShapeDtypeStruct((total, 2 * hidden), BF16) for _ in plans],
        scratch_shapes=[pltpu.VMEM((total, 2 * hidden), F32), pltpu.VMEM(acc.shape, F32)],
        compiler_params=pltpu.CompilerParams(vmem_limit_bytes=VMEM_LIMIT),
        name="far_gated",
    )(near_rows, acc, clean, *xs, *tables)


def down_step(hidden_rows, weights, first, count):
    def body(h_ref, w_ref, out_ref):
        out_ref[...] = jnp.dot(
            h_ref[pl.ds(first, count), :], w_ref[...], preferred_element_type=F32
        ).astype(BF16)

    return pl.pallas_call(
        body,
        in_specs=[whole(), whole()],
        out_specs=whole(),
        out_shape=jax.ShapeDtypeStruct((count, weights.shape[1]), BF16),
        compiler_params=pltpu.CompilerParams(vmem_limit_bytes=VMEM_LIMIT),
        name="down",
    )(hidden_rows, weights)


def local(tokens, group_ids, gates, w_in, w_down):
    groups, parts = lax.axis_size("grp"), lax.axis_size("exp")
    rows, features = tokens.shape
    hidden = w_in.shape[3]
    group_bits, part_bits = bits_of(groups), bits_of(parts)
    w_view = (
        w_in.reshape(2, features, 2, hidden // LANES, LANES)
        .transpose(0, 1, 3, 2, 4)
        .reshape(2, -1, LANES)
    )
    w_flat = w_down.reshape(2 * hidden, features)
    unit = features // 7

    def far(x):
        held = {0: x}
        for bit in reversed(range(1, group_bits)):
            for r in list(held):
                held[r | 1 << bit] = exchange(held[r], "grp", 1 << bit)
        return [held[r] for r in range(2, groups, 2)]

    def both(held):
        return held + [exchange(x, "grp", 1) for x in held]

    def both(held):
        return held + [exchange(x, "grp", 1) for x in held]

    run, steps = features // 14 * RUN, features // unit
    beside = exchange(tokens, "grp", 1)
    relayed, direct, table = prepare(tokens, group_ids, gates, run)
    relayed = far(relayed)
    table_beside = exchange(table, "grp", 1)
    held = [tokens, beside]
    spans = split(features, features // 28, [share for share, _ in CHUNKS])
    near = near_step(held, w_view, None, hidden, unit, 0, FRONT)
    direct = far(after(direct, near[0]))
    relayed, near = lax.optimization_barrier((relayed, near))
    passed = [exchange(x, "exp", 1) for x in relayed]
    near_acc, clean, *w_flats = near_step(
        held, w_view, near, hidden, unit, FRONT, steps, w_flat, spans
    )
    near_rows = near_gated(near_acc, [table, table_beside], hidden)
    direct, near_rows = lax.optimization_barrier((direct, near_rows))
    direct = both(direct)
    far_acc = far_step(None, clean, [both(relayed)], [(0, 0, 0, run, run)])
    passed, far_acc = lax.optimization_barrier((passed, far_acc))
    passed = both(passed)
    far_acc = far_step(far_acc, clean, [direct], [(0, 0, 2 * run, features - 2 * run, 0)])
    passed[-1] = after(passed[-1], far_acc)

    grp_stages = [("grp", b) for b in range(1, group_bits)]
    exp_stages = [("exp", b) for b in range(part_bits)]
    turned = exp_stages[::-1]
    by_name = {
        "yz": grp_stages + exp_stages,
        "yZ": grp_stages + turned,
        "zyz": exp_stages[:1] + grp_stages + exp_stages[1:],
        "Zyz": turned[:1] + grp_stages + turned[1:],
    }
    plans = [[by_name[name] for name in names] for _, names in CHUNKS]
    order = [0, 1] + list(range(2, groups, 2)) + list(range(3, groups, 2))
    last_parts = [(0, 0, run, run, -run)]
    all_rows = far_gated(
        near_rows, far_acc, clean, [passed], last_parts, direct, hidden, plans, order
    )

    def turn(x, routes, stage):
        pairs = []
        for g in range(groups):
            for e in range(parts):
                axis, bit = routes[g % 2][stage]
                to_g, to_e = (g ^ 1 << bit, e) if axis == "grp" else (g, e ^ 1 << bit)
                pairs.append((g * parts + e, to_g * parts + to_e))
        return lax.ppermute(x, ("grp", "exp"), pairs)

    state = []
    half = rows * groups // 2
    done = None
    for weights, plan_rows in zip(w_flats, all_rows):
        plan_rows = plan_rows if done is None else after(plan_rows, done)
        done = down_step(plan_rows, weights, half, half)
        state.append([exchange(done, "grp", 1)])
    for weights, plan_rows, terms in zip(w_flats, all_rows, state):
        done = down_step(after(plan_rows, done), weights, 0, half)
        terms.append(done)
    send = None
    height = half
    for stage in range(len(grp_stages + exp_stages)):
        height //= 2
        for terms, routes in zip(state, plans):
            if send is not None:
                terms[-1] = after(terms[-1], send)
            send = add(*[t[height : 2 * height] for t in terms])
            terms.append(turn(send, routes, stage))
    outs = []
    for terms in state:
        if outs:
            terms[-1] = after(terms[-1], outs[-1])
        outs.append(add(*[t[:height] for t in terms]))
    return jnp.concatenate(outs, axis=1)


def solution(mesh):
    in_specs = (
        P(("rep", "grp"), None),
        P(("rep", "grp"), None),
        P(("rep", "grp"), None),
        P("grp", None, None, "exp"),
        P("grp", "exp", None),
    )
    out_specs = P(("rep", "grp", "exp"), None)
    return jax.shard_map(local, mesh=mesh, in_specs=in_specs, out_specs=out_specs, check_vma=False)
```

```python
import jax
import jax.numpy as jnp
from jax import lax
from jax.experimental import pallas as pl
from jax.experimental.pallas import tpu as pltpu
from jax.sharding import PartitionSpec as P

F32 = jnp.float32
BF16 = jnp.bfloat16
LANES = 128
VMEM_LIMIT = 16 << 20
NEAR_COST = 3_000_000_000
RUN = 4
FRONT = 3
CHUNKS = [(17, ('yZ', 'zyz')), (11, ('yz', 'Zyz'))]


def bits_of(count):
    bits = count.bit_length() - 1
    assert 1 << bits == count
    return bits


def bit_reverse(value, bits):
    return sum(((value >> b) & 1) << (bits - 1 - b) for b in range(bits))


def exchange(x, axis, mask):
    return lax.ppermute(x, axis, [(i, i ^ mask) for i in range(lax.axis_size(axis))])


def add(*terms):
    return sum(t.astype(F32) for t in terms).astype(BF16)


def split(total, unit, shares):
    edges, whole = [0], total // unit
    for i in range(len(shares)):
        edges.append(round(whole * sum(shares[: i + 1]) / sum(shares)) * unit)
    return [(a, b - a) for a, b in zip(edges, edges[1:]) if b > a]


def after(x, *earlier):
    return lax.optimization_barrier((x, earlier))[0]


def prepare(tokens, group_ids, gates, relayed):
    rows, top = group_ids.shape
    direct = tokens.shape[1] - 2 * relayed

    def body(tokens_ref, ids_ref, gates_ref, first, second, table_ref, ids, weights, sems):
        start = pl.multiple_of((lax.axis_index("exp") % 2) * relayed, LANES)
        moves = [
            (ids_ref, ids),
            (gates_ref, weights),
            (tokens_ref.at[:, pl.ds(start, relayed)], first),
            (tokens_ref.at[:, pl.ds(2 * relayed, direct)], second.at[:, pl.ds(0, direct)]),
        ]
        copies = [pltpu.make_async_copy(*move, sems.at[i]) for i, move in enumerate(moves)]
        for copy in copies:
            copy.start()
        for copy in copies[:2]:
            copy.wait()
        expert = lax.broadcasted_iota(jnp.int32, (LANES, rows), 0)
        table = jnp.zeros((LANES, rows), F32)
        for k in range(top):
            even = weights[pl.ds(2 * k, 1), :].astype(F32)
            odd = weights[pl.ds(2 * k + 1, 1), :].astype(F32)
            gate = jnp.where(expert % 2 == 0, even, odd)
            table = jnp.where(expert // 2 == ids[pl.ds(k, 1), :], gate, table)
        table = table.T.astype(BF16)
        table_ref[...] = table
        second[:, pl.ds(direct, LANES)] = table
        for copy in copies[2:]:
            copy.wait()

    widths = [relayed, direct + LANES, LANES]
    return pl.pallas_call(
        body,
        in_specs=[whole(pl.ANY)] * 3,
        out_specs=[whole()] * 3,
        out_shape=[jax.ShapeDtypeStruct((rows, width), BF16) for width in widths],
        scratch_shapes=[
            pltpu.VMEM((top, rows), jnp.int32),
            pltpu.VMEM((2 * top, rows), BF16),
            pltpu.SemaphoreType.DMA((4,)),
        ],
        compiler_params=pltpu.CompilerParams(vmem_limit_bytes=VMEM_LIMIT),
        name="prepare",
    )(in_hbm(tokens), in_hbm(group_ids.T), in_hbm(gates.T))


def in_hbm(x):
    return pltpu.with_memory_space_constraint(x, pltpu.HBM)


def whole(memory_space=pltpu.VMEM):
    return pl.BlockSpec(memory_space=memory_space)


def near_step(xs, w_view, before, hidden, depth, first, last, extra=None, spans=()):
    rows, ratio = xs[0].shape[0], 2 * hidden // LANES
    halves, steps = hidden // LANES, last - first

    def body(*refs):
        x_refs, refs = refs[: len(xs)], list(refs[len(xs) :])
        w_ref = refs.pop(0)
        if extra is not None:
            extra_ref = refs.pop(0)
        if before is not None:
            before_ref, made_ref = refs.pop(0), refs.pop(0)
        acc_ref, clean_ref = refs.pop(0), refs.pop(0)
        extra_outs = [refs.pop(0) for _ in spans]
        held, blocks, sems = refs
        own = [
            pltpu.make_async_copy(
                ref.at[:, pl.ds(first * depth, steps * depth)],
                held.at[pl.ds(i * rows, rows), :],
                sems.at[i],
            )
            for i, ref in enumerate(x_refs)
        ]

        def fetch(step):
            return pltpu.make_async_copy(
                w_ref.at[:, pl.ds((first + step) * depth * ratio, depth * ratio), :],
                blocks.at[step],
                sems.at[len(xs) + step],
            )

        pieces = [
            pltpu.make_async_copy(
                extra_ref.at[:, pl.ds(*span)], out, sems.at[len(xs) + steps + i]
            )
            for i, (span, out) in enumerate(zip(spans, extra_outs))
        ]
        fetch(0).start()
        for copy in own:
            copy.start()
        for step in range(1, steps):
            fetch(step).start()
        for copy in pieces:
            copy.start()
        if before is not None:
            for step in range(first):
                here = pl.ds(step * depth, depth)
                clean_ref[here, :] = made_ref[here, :]
        for step in range(steps):
            fetch(step).wait()
            here = pl.ds((first + step) * depth, depth)
            for member in range(2):
                for s in range(2):
                    for t in range(halves):
                        column = (2 * member + s) * hidden + t * LANES
                        clean_ref[here, pl.ds(column, LANES)] = blocks[
                            step, member, pl.ds(2 * t + s, depth, stride=2 * halves), :
                        ]
            if step == 0:
                for copy in own:
                    copy.wait()
            value = jnp.dot(
                held[:, pl.ds(step * depth, depth)],
                clean_ref[here, :],
                preferred_element_type=F32,
            )
            if step or before is not None:
                value += (acc_ref if step else before_ref)[...]
            acc_ref[...] = value
        for copy in pieces:
            copy.wait()

    operands = [in_hbm(xs[0]), *xs[1:], in_hbm(w_view)]
    specs = [whole(pl.ANY)] * len(operands)
    if extra is not None:
        operands.append(in_hbm(extra))
        specs.append(whole(pl.ANY))
    if before is not None:
        operands += before
        specs += [whole()] * 2
    shapes = [
        jax.ShapeDtypeStruct((len(xs) * rows, 4 * hidden), F32),
        jax.ShapeDtypeStruct((last * depth, 4 * hidden), BF16),
    ]
    for _, width in spans:
        shapes.append(jax.ShapeDtypeStruct((extra.shape[0], width), extra.dtype))
    return pl.pallas_call(
        body,
        in_specs=specs,
        out_specs=[whole()] * len(shapes),
        out_shape=shapes,
        scratch_shapes=[
            pltpu.VMEM((len(xs) * rows, steps * depth), BF16),
            pltpu.VMEM((steps, 2, depth * ratio, LANES), BF16),
            pltpu.SemaphoreType.DMA((len(xs) + steps + len(spans),)),
        ],
        compiler_params=pltpu.CompilerParams(vmem_limit_bytes=VMEM_LIMIT),
        cost_estimate=pl.CostEstimate(
            flops=NEAR_COST, bytes_accessed=NEAR_COST // 300, transcendentals=0
        ),
        name="near",
    )(*operands)


def add_far(value, clean_ref, x_refs, parts, count):
    for which, column, start, depth, shift in parts:
        refs = x_refs[which * count : (which + 1) * count]
        if shift:
            start = pl.multiple_of(start + (lax.axis_index("exp") % 2) * shift, LANES)
        x = jnp.concatenate([ref[:, pl.ds(column, depth)] for ref in refs], axis=0)
        term = jnp.dot(x, clean_ref[pl.ds(start, depth), :], preferred_element_type=F32)
        value = term if value is None else value + term
    return value


def far_step(before, clean, blocks, parts):
    rows, count = blocks[0][0].shape[0], len(blocks[0])
    first = [] if before is None else [before]

    def body(*refs):
        value = None if before is None else refs[0][...]
        clean_ref, x_refs = refs[len(first)], refs[len(first) + 1 : -1]
        refs[-1][...] = add_far(value, clean_ref, x_refs, parts, count)

    operands = first + [clean] + [x for xs in blocks for x in xs]
    return pl.pallas_call(
        body,
        in_specs=[whole()] * len(operands),
        out_specs=whole(),
        out_shape=jax.ShapeDtypeStruct((count * rows, clean.shape[1]), F32),
        compiler_params=pltpu.CompilerParams(vmem_limit_bytes=VMEM_LIMIT),
        name="far",
    )(*operands)


def activate(acc, tables_ref, hidden):
    rows, group = tables_ref[0].shape[0], lax.axis_index("grp")
    lane = lax.broadcasted_iota(jnp.int32, (rows, LANES), 1)
    blocks = []
    for block, table_ref in enumerate(tables_ref):
        table = table_ref[...].astype(F32)
        members = []
        for member in range(2):
            chosen = jnp.where(lane == 2 * group + member, table, 0.0)
            gate = jnp.sum(chosen, axis=1, keepdims=True)
            both = acc[pl.ds(block * rows, rows), pl.ds(2 * member * hidden, 2 * hidden)]
            a, b = both[:, :hidden], both[:, hidden:]
            members.append(gate * (jax.nn.silu(a) * b))
        blocks.append(jnp.concatenate(members, axis=1))
    return jnp.concatenate(blocks, axis=0)


def table_specs(tables):
    return [
        pl.BlockSpec((t.shape[0], LANES), lambda i, c=t.shape[1] // LANES - 1: (0, c))
        for t in tables
    ]


def near_gated(acc, tables, hidden):
    def body(acc_ref, *refs):
        refs[-1][...] = activate(acc_ref, refs[:-1], hidden)

    return pl.pallas_call(
        body,
        grid=(1,),
        in_specs=[whole()] + table_specs(tables),
        out_specs=whole(),
        out_shape=jax.ShapeDtypeStruct((acc.shape[0], 2 * hidden), F32),
        compiler_params=pltpu.CompilerParams(vmem_limit_bytes=VMEM_LIMIT),
        name="near_gated",
    )(acc, *tables)


def far_gated(near_rows, acc, clean, blocks, far_parts, tables, hidden, plans, order):
    rows, count = tables[0].shape[0], near_rows.shape[0]
    total = count + acc.shape[0]
    parts = 1 << sum(axis == "exp" for axis, _ in plans[0][0])
    part, bits = rows // parts, len(plans[0][0])
    at_of = {r: i for i, r in enumerate(order)}
    xs = [x for block in blocks for x in block]

    def body(near_ref, acc_ref, clean_ref, *refs):
        x_refs, refs = refs[: len(xs)], refs[len(xs) :]
        table_refs, outs, (work, sums) = refs[: len(tables)], refs[len(tables) : -2], refs[-2:]
        sums[...] = add_far(acc_ref[...], clean_ref, x_refs, far_parts, len(blocks[0]))
        work[pl.ds(0, count), :] = near_ref[...]
        work[pl.ds(count, total - count), :] = activate(sums, table_refs, hidden)
        core, slot = lax.axis_index("grp") % 2, lax.axis_index("exp")
        for routes, out_ref in zip(plans, outs):
            for other in range(2):
                owner = (core + other) % 2
                pieces = []
                for p in range(1 << bits):
                    starts = []
                    for stages in routes:
                        rel = {"grp": other, "exp": 0}
                        for k, (axis, bit) in enumerate(stages):
                            rel[axis] |= ((p >> (bits - 1 - k)) & 1) << bit
                        place = jnp.bitwise_xor(slot, rel["exp"]) * part
                        starts.append(at_of[rel["grp"]] * rows + place)
                    start = jnp.where(owner == 0, *starts)
                    pieces.append(work[pl.ds(pl.multiple_of(start, part), part), :])
                out_ref[pl.ds(other * (total // 2), total // 2), :] = jnp.concatenate(
                    pieces, axis=0
                ).astype(BF16)

    return pl.pallas_call(
        body,
        grid=(1,),
        in_specs=[whole()] * (3 + len(xs)) + table_specs(tables),
        out_specs=[whole() for _ in plans],
        out_shape=[jax.ShapeDtypeStruct((total, 2 * hidden), BF16) for _ in plans],
        scratch_shapes=[pltpu.VMEM((total, 2 * hidden), F32), pltpu.VMEM(acc.shape, F32)],
        compiler_params=pltpu.CompilerParams(vmem_limit_bytes=VMEM_LIMIT),
        name="far_gated",
    )(near_rows, acc, clean, *xs, *tables)


def down_step(hidden_rows, weights, first, count):
    def body(h_ref, w_ref, out_ref):
        out_ref[...] = jnp.dot(
            h_ref[pl.ds(first, count), :], w_ref[...], preferred_element_type=F32
        ).astype(BF16)

    return pl.pallas_call(
        body,
        in_specs=[whole(), whole()],
        out_specs=whole(),
        out_shape=jax.ShapeDtypeStruct((count, weights.shape[1]), BF16),
        compiler_params=pltpu.CompilerParams(vmem_limit_bytes=VMEM_LIMIT),
        name="down",
    )(hidden_rows, weights)


def local(tokens, group_ids, gates, w_in, w_down):
    groups, parts = lax.axis_size("grp"), lax.axis_size("exp")
    rows, features = tokens.shape
    hidden = w_in.shape[3]
    group_bits, part_bits = bits_of(groups), bits_of(parts)
    w_view = (
        w_in.reshape(2, features, 2, hidden // LANES, LANES)
        .transpose(0, 1, 3, 2, 4)
        .reshape(2, -1, LANES)
    )
    w_flat = w_down.reshape(2 * hidden, features)
    unit = features // 7

    def far(x):
        held = {0: x}
        for bit in reversed(range(1, group_bits)):
            for r in list(held):
                held[r | 1 << bit] = exchange(held[r], "grp", 1 << bit)
        return [held[r] for r in range(2, groups, 2)]

    def both(held):
        return held + [exchange(x, "grp", 1) for x in held]

    def both(held):
        return held + [exchange(x, "grp", 1) for x in held]

    run, steps = features // 14 * RUN, features // unit
    beside = exchange(tokens, "grp", 1)
    relayed, direct, table = prepare(tokens, group_ids, gates, run)
    relayed = far(relayed)
    table_beside = exchange(table, "grp", 1)
    held = [tokens, beside]
    spans = split(features, features // 28, [share for share, _ in CHUNKS])
    near = near_step(held, w_view, None, hidden, unit, 0, FRONT)
    direct = far(after(direct, near[0]))
    relayed, near = lax.optimization_barrier((relayed, near))
    passed = [exchange(x, "exp", 1) for x in relayed]
    near_acc, clean, *w_flats = near_step(
        held, w_view, near, hidden, unit, FRONT, steps, w_flat, spans
    )
    near_rows = near_gated(near_acc, [table, table_beside], hidden)
    direct, near_rows = lax.optimization_barrier((direct, near_rows))
    direct = both(direct)
    far_acc = far_step(None, clean, [both(relayed)], [(0, 0, 0, run, run)])
    passed, far_acc = lax.optimization_barrier((passed, far_acc))
    passed = both(passed)
    far_acc = far_step(far_acc, clean, [direct], [(0, 0, 2 * run, features - 2 * run, 0)])
    passed[-1] = after(passed[-1], far_acc)

    grp_stages = [("grp", b) for b in range(1, group_bits)]
    exp_stages = [("exp", b) for b in range(part_bits)]
    turned = exp_stages[::-1]
    by_name = {
        "yz": grp_stages + exp_stages,
        "yZ": grp_stages + turned,
        "zyz": exp_stages[:1] + grp_stages + exp_stages[1:],
        "Zyz": turned[:1] + grp_stages + turned[1:],
    }
    plans = [[by_name[name] for name in names] for _, names in CHUNKS]
    order = [0, 1] + list(range(2, groups, 2)) + list(range(3, groups, 2))
    last_parts = [(0, 0, run, run, -run)]
    all_rows = far_gated(
        near_rows, far_acc, clean, [passed], last_parts, direct, hidden, plans, order
    )

    def turn(x, routes, stage):
        pairs = []
        for g in range(groups):
            for e in range(parts):
                axis, bit = routes[g % 2][stage]
                to_g, to_e = (g ^ 1 << bit, e) if axis == "grp" else (g, e ^ 1 << bit)
                pairs.append((g * parts + e, to_g * parts + to_e))
        return lax.ppermute(x, ("grp", "exp"), pairs)

    state = []
    half = rows * groups // 2
    done = None
    for weights, plan_rows in zip(w_flats, all_rows):
        plan_rows = plan_rows if done is None else after(plan_rows, done)
        done = down_step(plan_rows, weights, half, half)
        state.append([exchange(done, "grp", 1)])
    for weights, plan_rows, terms in zip(w_flats, all_rows, state):
        done = down_step(after(plan_rows, done), weights, 0, half)
        terms.append(done)
    send = None
    height = half
    for stage in range(len(grp_stages + exp_stages)):
        height //= 2
        for terms, routes in zip(state, plans):
            if send is not None:
                terms[-1] = after(terms[-1], send)
            send = add(*[t[height : 2 * height] for t in terms])
            terms.append(turn(send, routes, stage))
    outs = []
    for terms in state:
        if outs:
            terms[-1] = after(terms[-1], outs[-1])
        outs.append(add(*[t[:height] for t in terms]))
    return jnp.concatenate(outs, axis=1)


def solution(mesh):
    in_specs = (
        P(("rep", "grp"), None),
        P(("rep", "grp"), None),
        P(("rep", "grp"), None),
        P("grp", None, None, "exp"),
        P("grp", "exp", None),
    )
    out_specs = P(("rep", "grp", "exp"), None)
    return jax.shard_map(local, mesh=mesh, in_specs=in_specs, out_specs=out_specs, check_vma=False)
```

```python
import jax
import jax.numpy as jnp
from jax import lax
from jax.experimental import pallas as pl
from jax.experimental.pallas import tpu as pltpu
from jax.sharding import PartitionSpec as P

F32 = jnp.float32
BF16 = jnp.bfloat16
LANES = 128
VMEM_LIMIT = 16 << 20
NEAR_COST = 3_000_000_000
RUN = 4
FRONT = 3
CHUNKS = [(17, ('yZ', 'zyz')), (11, ('yz', 'Zyz'))]


def bits_of(count):
    bits = count.bit_length() - 1
    assert 1 << bits == count
    return bits


def bit_reverse(value, bits):
    return sum(((value >> b) & 1) << (bits - 1 - b) for b in range(bits))


def exchange(x, axis, mask):
    return lax.ppermute(x, axis, [(i, i ^ mask) for i in range(lax.axis_size(axis))])


def add(*terms):
    return sum(t.astype(F32) for t in terms).astype(BF16)


def split(total, unit, shares):
    edges, whole = [0], total // unit
    for i in range(len(shares)):
        edges.append(round(whole * sum(shares[: i + 1]) / sum(shares)) * unit)
    return [(a, b - a) for a, b in zip(edges, edges[1:]) if b > a]


def after(x, *earlier):
    return lax.optimization_barrier((x, earlier))[0]


def prepare(tokens, group_ids, gates, relayed):
    rows, top = group_ids.shape
    direct = tokens.shape[1] - 2 * relayed

    def body(tokens_ref, ids_ref, gates_ref, first, second, table_ref, ids, weights, sems):
        start = pl.multiple_of((lax.axis_index("exp") % 2) * relayed, LANES)
        moves = [
            (ids_ref, ids),
            (gates_ref, weights),
            (tokens_ref.at[:, pl.ds(start, relayed)], first),
            (tokens_ref.at[:, pl.ds(2 * relayed, direct)], second.at[:, pl.ds(0, direct)]),
        ]
        copies = [pltpu.make_async_copy(*move, sems.at[i]) for i, move in enumerate(moves)]
        for copy in copies:
            copy.start()
        for copy in copies[:2]:
            copy.wait()
        expert = lax.broadcasted_iota(jnp.int32, (LANES, rows), 0)
        table = jnp.zeros((LANES, rows), F32)
        for k in range(top):
            even = weights[pl.ds(2 * k, 1), :].astype(F32)
            odd = weights[pl.ds(2 * k + 1, 1), :].astype(F32)
            gate = jnp.where(expert % 2 == 0, even, odd)
            table = jnp.where(expert // 2 == ids[pl.ds(k, 1), :], gate, table)
        table = table.T.astype(BF16)
        table_ref[...] = table
        second[:, pl.ds(direct, LANES)] = table
        for copy in copies[2:]:
            copy.wait()

    widths = [relayed, direct + LANES, LANES]
    return pl.pallas_call(
        body,
        in_specs=[whole(pl.ANY)] * 3,
        out_specs=[whole()] * 3,
        out_shape=[jax.ShapeDtypeStruct((rows, width), BF16) for width in widths],
        scratch_shapes=[
            pltpu.VMEM((top, rows), jnp.int32),
            pltpu.VMEM((2 * top, rows), BF16),
            pltpu.SemaphoreType.DMA((4,)),
        ],
        compiler_params=pltpu.CompilerParams(vmem_limit_bytes=VMEM_LIMIT),
        name="prepare",
    )(in_hbm(tokens), in_hbm(group_ids.T), in_hbm(gates.T))


def in_hbm(x):
    return pltpu.with_memory_space_constraint(x, pltpu.HBM)


def whole(memory_space=pltpu.VMEM):
    return pl.BlockSpec(memory_space=memory_space)


def near_step(xs, w_view, before, hidden, depth, first, last, extra=None, spans=()):
    rows, ratio = xs[0].shape[0], 2 * hidden // LANES
    halves, steps = hidden // LANES, last - first

    def body(*refs):
        x_refs, refs = refs[: len(xs)], list(refs[len(xs) :])
        w_ref = refs.pop(0)
        if extra is not None:
            extra_ref = refs.pop(0)
        if before is not None:
            before_ref, made_ref = refs.pop(0), refs.pop(0)
        acc_ref, clean_ref = refs.pop(0), refs.pop(0)
        extra_outs = [refs.pop(0) for _ in spans]
        held, blocks, sems = refs
        own = [
            pltpu.make_async_copy(
                ref.at[:, pl.ds(first * depth, steps * depth)],
                held.at[pl.ds(i * rows, rows), :],
                sems.at[i],
            )
            for i, ref in enumerate(x_refs)
        ]

        def fetch(step):
            return pltpu.make_async_copy(
                w_ref.at[:, pl.ds((first + step) * depth * ratio, depth * ratio), :],
                blocks.at[step],
                sems.at[len(xs) + step],
            )

        pieces = [
            pltpu.make_async_copy(
                extra_ref.at[:, pl.ds(*span)], out, sems.at[len(xs) + steps + i]
            )
            for i, (span, out) in enumerate(zip(spans, extra_outs))
        ]
        fetch(0).start()
        for copy in own:
            copy.start()
        for step in range(1, steps):
            fetch(step).start()
        for copy in pieces:
            copy.start()
        if before is not None:
            for step in range(first):
                here = pl.ds(step * depth, depth)
                clean_ref[here, :] = made_ref[here, :]
        for step in range(steps):
            fetch(step).wait()
            here = pl.ds((first + step) * depth, depth)
            for member in range(2):
                for s in range(2):
                    for t in range(halves):
                        column = (2 * member + s) * hidden + t * LANES
                        clean_ref[here, pl.ds(column, LANES)] = blocks[
                            step, member, pl.ds(2 * t + s, depth, stride=2 * halves), :
                        ]
            if step == 0:
                for copy in own:
                    copy.wait()
            value = jnp.dot(
                held[:, pl.ds(step * depth, depth)],
                clean_ref[here, :],
                preferred_element_type=F32,
            )
            if step or before is not None:
                value += (acc_ref if step else before_ref)[...]
            acc_ref[...] = value
        for copy in pieces:
            copy.wait()

    operands = [in_hbm(xs[0]), *xs[1:], in_hbm(w_view)]
    specs = [whole(pl.ANY)] * len(operands)
    if extra is not None:
        operands.append(in_hbm(extra))
        specs.append(whole(pl.ANY))
    if before is not None:
        operands += before
        specs += [whole()] * 2
    shapes = [
        jax.ShapeDtypeStruct((len(xs) * rows, 4 * hidden), F32),
        jax.ShapeDtypeStruct((last * depth, 4 * hidden), BF16),
    ]
    for _, width in spans:
        shapes.append(jax.ShapeDtypeStruct((extra.shape[0], width), extra.dtype))
    return pl.pallas_call(
        body,
        in_specs=specs,
        out_specs=[whole()] * len(shapes),
        out_shape=shapes,
        scratch_shapes=[
            pltpu.VMEM((len(xs) * rows, steps * depth), BF16),
            pltpu.VMEM((steps, 2, depth * ratio, LANES), BF16),
            pltpu.SemaphoreType.DMA((len(xs) + steps + len(spans),)),
        ],
        compiler_params=pltpu.CompilerParams(vmem_limit_bytes=VMEM_LIMIT),
        cost_estimate=pl.CostEstimate(
            flops=NEAR_COST, bytes_accessed=NEAR_COST // 300, transcendentals=0
        ),
        name="near",
    )(*operands)


def add_far(value, clean_ref, x_refs, parts, count):
    for which, column, start, depth, shift in parts:
        refs = x_refs[which * count : (which + 1) * count]
        if shift:
            start = pl.multiple_of(start + (lax.axis_index("exp") % 2) * shift, LANES)
        x = jnp.concatenate([ref[:, pl.ds(column, depth)] for ref in refs], axis=0)
        term = jnp.dot(x, clean_ref[pl.ds(start, depth), :], preferred_element_type=F32)
        value = term if value is None else value + term
    return value


def far_step(before, clean, blocks, parts):
    rows, count = blocks[0][0].shape[0], len(blocks[0])
    first = [] if before is None else [before]

    def body(*refs):
        value = None if before is None else refs[0][...]
        clean_ref, x_refs = refs[len(first)], refs[len(first) + 1 : -1]
        refs[-1][...] = add_far(value, clean_ref, x_refs, parts, count)

    operands = first + [clean] + [x for xs in blocks for x in xs]
    return pl.pallas_call(
        body,
        in_specs=[whole()] * len(operands),
        out_specs=whole(),
        out_shape=jax.ShapeDtypeStruct((count * rows, clean.shape[1]), F32),
        compiler_params=pltpu.CompilerParams(vmem_limit_bytes=VMEM_LIMIT),
        name="far",
    )(*operands)


def activate(acc, tables_ref, hidden):
    rows, group = tables_ref[0].shape[0], lax.axis_index("grp")
    lane = lax.broadcasted_iota(jnp.int32, (rows, LANES), 1)
    blocks = []
    for block, table_ref in enumerate(tables_ref):
        table = table_ref[...].astype(F32)
        members = []
        for member in range(2):
            chosen = jnp.where(lane == 2 * group + member, table, 0.0)
            gate = jnp.sum(chosen, axis=1, keepdims=True)
            both = acc[pl.ds(block * rows, rows), pl.ds(2 * member * hidden, 2 * hidden)]
            a, b = both[:, :hidden], both[:, hidden:]
            members.append(gate * (jax.nn.silu(a) * b))
        blocks.append(jnp.concatenate(members, axis=1))
    return jnp.concatenate(blocks, axis=0)


def table_specs(tables):
    return [
        pl.BlockSpec((t.shape[0], LANES), lambda i, c=t.shape[1] // LANES - 1: (0, c))
        for t in tables
    ]


def near_gated(acc, tables, hidden):
    def body(acc_ref, *refs):
        refs[-1][...] = activate(acc_ref, refs[:-1], hidden)

    return pl.pallas_call(
        body,
        grid=(1,),
        in_specs=[whole()] + table_specs(tables),
        out_specs=whole(),
        out_shape=jax.ShapeDtypeStruct((acc.shape[0], 2 * hidden), F32),
        compiler_params=pltpu.CompilerParams(vmem_limit_bytes=VMEM_LIMIT),
        name="near_gated",
    )(acc, *tables)


def far_gated(near_rows, acc, clean, blocks, far_parts, tables, hidden, plans, order):
    rows, count = tables[0].shape[0], near_rows.shape[0]
    total = count + acc.shape[0]
    parts = 1 << sum(axis == "exp" for axis, _ in plans[0][0])
    part, bits = rows // parts, len(plans[0][0])
    at_of = {r: i for i, r in enumerate(order)}
    xs = [x for block in blocks for x in block]

    def body(near_ref, acc_ref, clean_ref, *refs):
        x_refs, refs = refs[: len(xs)], refs[len(xs) :]
        table_refs, outs, (work, sums) = refs[: len(tables)], refs[len(tables) : -2], refs[-2:]
        sums[...] = add_far(acc_ref[...], clean_ref, x_refs, far_parts, len(blocks[0]))
        work[pl.ds(0, count), :] = near_ref[...]
        work[pl.ds(count, total - count), :] = activate(sums, table_refs, hidden)
        core, slot = lax.axis_index("grp") % 2, lax.axis_index("exp")
        for routes, out_ref in zip(plans, outs):
            for other in range(2):
                owner = (core + other) % 2
                pieces = []
                for p in range(1 << bits):
                    starts = []
                    for stages in routes:
                        rel = {"grp": other, "exp": 0}
                        for k, (axis, bit) in enumerate(stages):
                            rel[axis] |= ((p >> (bits - 1 - k)) & 1) << bit
                        place = jnp.bitwise_xor(slot, rel["exp"]) * part
                        starts.append(at_of[rel["grp"]] * rows + place)
                    start = jnp.where(owner == 0, *starts)
                    pieces.append(work[pl.ds(pl.multiple_of(start, part), part), :])
                out_ref[pl.ds(other * (total // 2), total // 2), :] = jnp.concatenate(
                    pieces, axis=0
                ).astype(BF16)

    return pl.pallas_call(
        body,
        grid=(1,),
        in_specs=[whole()] * (3 + len(xs)) + table_specs(tables),
        out_specs=[whole() for _ in plans],
        out_shape=[jax.ShapeDtypeStruct((total, 2 * hidden), BF16) for _ in plans],
        scratch_shapes=[pltpu.VMEM((total, 2 * hidden), F32), pltpu.VMEM(acc.shape, F32)],
        compiler_params=pltpu.CompilerParams(vmem_limit_bytes=VMEM_LIMIT),
        name="far_gated",
    )(near_rows, acc, clean, *xs, *tables)


def down_step(hidden_rows, weights, first, count):
    def body(h_ref, w_ref, out_ref):
        out_ref[...] = jnp.dot(
            h_ref[pl.ds(first, count), :], w_ref[...], preferred_element_type=F32
        ).astype(BF16)

    return pl.pallas_call(
        body,
        in_specs=[whole(), whole()],
        out_specs=whole(),
        out_shape=jax.ShapeDtypeStruct((count, weights.shape[1]), BF16),
        compiler_params=pltpu.CompilerParams(vmem_limit_bytes=VMEM_LIMIT),
        name="down",
    )(hidden_rows, weights)


def finish(state, rows):
    counts = [len(terms) for terms in state]

    def body(*refs):
        refs, out_ref = list(refs[:-1]), refs[-1]
        start = 0
        for count in counts:
            terms, refs = refs[:count], refs[count:]
            width = terms[0].shape[1]
            total = sum(ref[...].astype(F32) for ref in terms)
            out_ref[:, pl.ds(start, width)] = total.astype(BF16)
            start += width

    operands = [t for terms in state for t in terms]
    width = sum(terms[0].shape[1] for terms in state)
    return pl.pallas_call(
        body,
        grid=(1,),
        in_specs=[pl.BlockSpec((rows, t.shape[1]), lambda i: (0, 0)) for t in operands],
        out_specs=whole(),
        out_shape=jax.ShapeDtypeStruct((rows, width), BF16),
        compiler_params=pltpu.CompilerParams(vmem_limit_bytes=VMEM_LIMIT),
        name="finish",
    )(*operands)


def local(tokens, group_ids, gates, w_in, w_down):
    groups, parts = lax.axis_size("grp"), lax.axis_size("exp")
    rows, features = tokens.shape
    hidden = w_in.shape[3]
    group_bits, part_bits = bits_of(groups), bits_of(parts)
    w_view = (
        w_in.reshape(2, features, 2, hidden // LANES, LANES)
        .transpose(0, 1, 3, 2, 4)
        .reshape(2, -1, LANES)
    )
    w_flat = w_down.reshape(2 * hidden, features)
    unit = features // 7

    def far(x):
        held = {0: x}
        for bit in reversed(range(1, group_bits)):
            for r in list(held):
                held[r | 1 << bit] = exchange(held[r], "grp", 1 << bit)
        return [held[r] for r in range(2, groups, 2)]

    def both(held):
        return held + [exchange(x, "grp", 1) for x in held]

    def both(held):
        return held + [exchange(x, "grp", 1) for x in held]

    run, steps = features // 14 * RUN, features // unit
    beside = exchange(tokens, "grp", 1)
    relayed, direct, table = prepare(tokens, group_ids, gates, run)
    relayed = far(relayed)
    table_beside = exchange(table, "grp", 1)
    held = [tokens, beside]
    spans = split(features, features // 28, [share for share, _ in CHUNKS])
    near = near_step(held, w_view, None, hidden, unit, 0, FRONT)
    direct = far(after(direct, near[0]))
    relayed, near = lax.optimization_barrier((relayed, near))
    passed = [exchange(x, "exp", 1) for x in relayed]
    near_acc, clean, *w_flats = near_step(
        held, w_view, near, hidden, unit, FRONT, steps, w_flat, spans
    )
    near_rows = near_gated(near_acc, [table, table_beside], hidden)
    direct, near_rows = lax.optimization_barrier((direct, near_rows))
    direct = both(direct)
    far_acc = far_step(None, clean, [both(relayed)], [(0, 0, 0, run, run)])
    passed, far_acc = lax.optimization_barrier((passed, far_acc))
    passed = both(passed)
    far_acc = far_step(far_acc, clean, [direct], [(0, 0, 2 * run, features - 2 * run, 0)])
    passed[-1] = after(passed[-1], far_acc)

    grp_stages = [("grp", b) for b in range(1, group_bits)]
    exp_stages = [("exp", b) for b in range(part_bits)]
    turned = exp_stages[::-1]
    by_name = {
        "yz": grp_stages + exp_stages,
        "yZ": grp_stages + turned,
        "zyz": exp_stages[:1] + grp_stages + exp_stages[1:],
        "Zyz": turned[:1] + grp_stages + turned[1:],
    }
    plans = [[by_name[name] for name in names] for _, names in CHUNKS]
    order = [0, 1] + list(range(2, groups, 2)) + list(range(3, groups, 2))
    last_parts = [(0, 0, run, run, -run)]
    all_rows = far_gated(
        near_rows, far_acc, clean, [passed], last_parts, direct, hidden, plans, order
    )

    def turn(x, routes, stage):
        pairs = []
        for g in range(groups):
            for e in range(parts):
                axis, bit = routes[g % 2][stage]
                to_g, to_e = (g ^ 1 << bit, e) if axis == "grp" else (g, e ^ 1 << bit)
                pairs.append((g * parts + e, to_g * parts + to_e))
        return lax.ppermute(x, ("grp", "exp"), pairs)

    half = rows * groups // 2
    (first_w, second_w), (first_rows, second_rows) = w_flats, all_rows
    send = down_step(first_rows, first_w, half, half)
    first_terms = [exchange(send, "grp", 1)]
    keep = down_step(after(first_rows, send), first_w, 0, half)
    first_terms.insert(0, keep)
    send = down_step(after(second_rows, keep), second_w, half, half)
    second_terms = [exchange(send, "grp", 1)]
    state = [first_terms, second_terms]
    send = None
    height = half
    for stage in range(len(grp_stages + exp_stages)):
        height //= 2
        for terms, routes in zip(state, plans):
            if len(terms) == 1:
                terms.insert(0, down_step(after(second_rows, send), second_w, 0, half))
            else:
                terms[-1] = after(terms[-1], send)
            send = add(*[t[height : 2 * height] for t in terms])
            terms.append(turn(send, routes, stage))
    return finish(state, height)


def solution(mesh):
    in_specs = (
        P(("rep", "grp"), None),
        P(("rep", "grp"), None),
        P(("rep", "grp"), None),
        P("grp", None, None, "exp"),
        P("grp", "exp", None),
    )
    out_specs = P(("rep", "grp", "exp"), None)
    return jax.shard_map(local, mesh=mesh, in_specs=in_specs, out_specs=out_specs, check_vma=False)
```
